32 devices in a mesh: dom: 8 (over z, x), rep: 4 (over y, core).
Axes of the slice: x: 2, y: 2, z: 4, core: 2. Of those that a mesh axis runs over, the one named last changes fastest.
Arguments:
- features: bfloat16 [32768, 1024], P(('dom', 'rep')), may hold values from -6 to 6
- node_type: int32 [32768], P(('dom', 'rep')), may hold values 0 or 1
- neighbours: int32 [32768, 50], P(('dom', 'rep')), may hold values from 0 to 1535, as said below
- importance: float32 [32768, 50], P(('dom', 'rep')), may hold values from 0 to 1, as said below
- send_rows: int32 [16384], P(('dom', 'rep')), may hold values from 0 to 1023, as said below
- live_rows: int32 [32], P(('dom', 'rep')), may hold values from 512 to 1024, as said below
- proj_board: bfloat16 [512, 1024], replicated, may hold values from -0.25 to 0.25
- q_weight: bfloat16 [1024, 1024], replicated, may hold values from -0.1875 to 0.1875
- q_bias: float32 [1024], replicated, may hold values from -3 to 3
- w_weight: bfloat16 [2048, 1024], replicated, may hold values from -0.125 to 0.125
- w_bias: float32 [1024], replicated, may hold values from -3 to 3
- cotangent: bfloat16 [32768, 1024], P(('dom', 'rep')), may hold values from -6 to 6
Outputs:
- embedding: float32 [32768, 1024], P(('dom', 'rep'))
- grad_features: float32 [32768, 1024], P(('dom', 'rep'))
- grad_proj: float32 [512, 1024], replicated
- grad_q: float32 [1024, 1024], replicated
- grad_q_bias: float32 [1024], replicated
- grad_w: float32 [2048, 1024], replicated
- grad_w_bias: float32 [1024], replicated
The draws below stay inside these ranges and needn't reach their ends.
Inputs may be any that keep to these rules, and one draw needn't show every extreme that they name: `live_rows`: live rows of a device lie between half of 1024 and 1024; the first device has all 1024 live. `send_rows`: every entry names a live row of the sending device; every peer receives exactly 64 rows. `neighbours`: Own-row entries name live rows; padded slots hold 0. `importance`: each node has at least one slot with a positive weight; padded slots weigh 0.
All inputs are finite; a program needn't handle non-finite values. No bound on the sum of `node_type` on one device may be relied on, other than what follows from the above.
Results may differ from the reference program's by a relative error of at most 0.0075.
Values may be sent and summed in bfloat16 or wider, within the bound.
No kernel may reach another device: no remote copies, remote signals or barrier semaphores. Data moves between devices by JAX's collectives and lax.ppermute only.
A program may use at most 192 MiB of HBM per device.

```python
import jax
import jax.numpy as jnp
from jax import lax

D = 1024
BOARD = 512
K = 50
NODE_DEV = 1024
SLOT = 64
HALO = 512
NODES = 32768
N_REP = 4


def live_counts(key):
    count = jax.random.randint(jax.random.fold_in(key, 11), (NODES // NODE_DEV,), NODE_DEV // 2, NODE_DEV + 1)
    return count.at[0].set(NODE_DEV).astype(jnp.int32)


def slot_counts(key):
    count = jax.random.randint(jax.random.fold_in(key, 13), (NODES // NODE_DEV, NODE_DEV), K // 5 + 1, K + 1)
    return count.at[:, 0].set(K).reshape(NODES)


def draw_live_rows(key, part):
    return live_counts(key)


def draw_send_rows(key, part):
    live = live_counts(key)
    raw = jax.random.randint(jax.random.fold_in(key, 12), (NODES // NODE_DEV, HALO), 0, 1 << 30)
    rows = raw % live[:, None]
    rows = rows.at[:, 0].set(live - 1)
    return rows.reshape(-1).astype(jnp.int32)


def draw_neighbours(key, part):
    live = live_counts(key)
    devices = NODES // NODE_DEV
    live_node = jnp.repeat(live, NODE_DEV)[:, None]
    raw = jax.random.randint(jax.random.fold_in(key, 14), (NODES, K), 0, 1 << 30)
    other = jax.random.randint(jax.random.fold_in(key, 15), (NODES, K), 0, 1 << 30)
    remote = jax.random.randint(jax.random.fold_in(key, 16), (NODES, K), 0, 10) < 3
    index = jnp.where(remote, NODE_DEV + other % HALO, raw % live_node)
    count = slot_counts(key)
    index = jnp.where(jnp.arange(K)[None, :] < count[:, None], index, 0)
    index = index.reshape(devices, NODE_DEV, K).at[:, 0, 0].set(NODE_DEV + HALO - 1)
    return index.reshape(NODES, K).astype(jnp.int32)


def draw_importance(key, part):
    count = slot_counts(key)
    level = jax.random.uniform(jax.random.fold_in(key, 17), (NODES, K), jnp.float32, jnp.log(0.1), 0.0)
    weight = jnp.exp(level)
    return jnp.where(jnp.arange(K)[None, :] < count[:, None], weight, 0.0).astype(jnp.float32)


def touch_ends(array, own_key, smallest, high):
    longest = array.shape.index(max(array.shape))
    spots = []
    for shift in (0, 1):
        where = [jax.random.randint(jax.random.fold_in(own_key, axis), (), 0, length) for axis, length in enumerate(array.shape)]
        where[longest] = (where[longest] + shift) % array.shape[longest]
        spots.append(tuple(where))
    return array.at[spots[0]].set(smallest).at[spots[1]].set(high)


def levels(own_key, extent, shards, low, top_value):
    gain = 1.0
    for position, parts in shards:
        steps = jax.random.uniform(jax.random.fold_in(jax.random.fold_in(own_key, 6), position), (parts,), jnp.float32, low / len(shards), top_value / len(shards))
        gain = gain * jnp.repeat(jnp.exp(steps), extent[position] // parts).reshape((-1,) + (1,) * (len(extent) - 1 - position))
    return gain


def noise(rng, dims, scale, reach, cuts=(), kind=jnp.bfloat16):
    values = scale * jax.random.normal(rng, dims, jnp.float32)
    if cuts:
        values = values * levels(rng, dims, cuts, -0.22, 0.18)
    return jnp.clip(values, -reach, reach).astype(kind)


def setup_inputs(seed: int = 0) -> dict:
    streams_of = jax.random.split(jax.random.key(seed), 13)
    features = noise(streams_of[0], (NODES, D), 1.0, 6.0, ((0, 32),))
    node_type = touch_ends((jax.random.randint(streams_of[1], (NODES,), 0, 2) < 1).astype(jnp.int32), jax.random.fold_in(streams_of[1], 1), 0, 1)
    neighbours = draw_neighbours(jax.random.fold_in(streams_of[12], 71), 0)
    importance = draw_importance(jax.random.fold_in(streams_of[12], 71), 0)
    send_rows = draw_send_rows(jax.random.fold_in(streams_of[12], 71), 0)
    live_rows = draw_live_rows(jax.random.fold_in(streams_of[12], 71), 0)
    proj_board = noise(streams_of[6], (BOARD, D), BOARD ** -0.5, 0.25)
    q_weight = noise(streams_of[7], (D, D), D ** -0.5, 0.1875)
    q_bias = noise(streams_of[8], (D,), 0.3, 3.0, (), jnp.float32)
    w_weight = noise(streams_of[9], (2 * D, D), (2 * D) ** -0.5, 0.125)
    w_bias = noise(streams_of[10], (D,), 0.3, 3.0, (), jnp.float32)
    cotangent = noise(streams_of[11], (NODES, D), 1.0, 6.0, ((0, 32),))
    return {"features": features, "node_type": node_type, "neighbours": neighbours, "importance": importance, "send_rows": send_rows, "live_rows": live_rows, "proj_board": proj_board, "q_weight": q_weight, "q_bias": q_bias, "w_weight": w_weight, "w_bias": w_bias, "cotangent": cotangent}


@jax.custom_vjp
def low(v):
    return lax.optimization_barrier(v.astype(jnp.bfloat16)).astype(jnp.float32)

@jax.custom_vjp
def low_back(v):
    return v

def low_keep(v):
    return (low(v), None)

def low_pass(kept, grad):
    return (grad,)

def back_keep(v):
    return (v, None)

def back_low(kept, grad):
    return (low(grad),)
low.defvjp(low_keep, low_pass)
low_back.defvjp(back_keep, back_low)

def reference(features, node_type, neighbours, importance, send_rows, live_rows, proj_board, q_weight, q_bias, w_weight, w_bias, cotangent):
    nodes = features.shape[0]
    device = jnp.arange(nodes, dtype=jnp.int32) // NODE_DEV
    dom_index = device // N_REP
    rep_index = device % N_REP
    is_local = neighbours < NODE_DEV
    offset = jnp.maximum(neighbours - NODE_DEV, 0)
    peer = offset // SLOT
    within = offset % SLOT
    sender = peer * N_REP + rep_index[:, None]
    sent_row = send_rows[sender * HALO + dom_index[:, None] * SLOT + within]
    source = jnp.where(is_local, device[:, None] * NODE_DEV + neighbours, sender * NODE_DEV + sent_row).astype(jnp.int32)
    live = (jnp.arange(nodes, dtype=jnp.int32) % NODE_DEV < live_rows[device])[:, None]
    board = (node_type == 1)[:, None]
    total = lax.optimization_barrier(jnp.sum(importance, axis=1, keepdims=True))
    hp = lax.Precision.HIGHEST

    def forward(feats, proj, qmat, qvec, wmat, wvec):
        projected = jnp.dot(feats[:, :BOARD], proj, precision=hp)
        hidden = low_back(low(jnp.where(board, projected, feats)))
        pre = low_back(jnp.dot(hidden, qmat, precision=hp) + qvec)
        active = low(jax.nn.silu(pre))

        def add_slot(carry, slot):
            index, weight = slot
            return (carry + weight[:, None] * active[index], None)
        agg, unused = lax.scan(add_slot, jnp.zeros((nodes, D), jnp.float32), (source.T, importance.T))
        mean = agg / total
        joined = jnp.concatenate([hidden, low(mean)], axis=1)
        pre2 = low_back(jnp.dot(joined, wmat, precision=hp) + wvec)
        post = jax.nn.silu(pre2)
        scale = lax.rsqrt(lax.optimization_barrier(jnp.sum(post * post, axis=1, keepdims=True)) + 1e-06)
        return jnp.where(live, post * scale, 0.0)
    primals = (features.astype(jnp.float32), proj_board.astype(jnp.float32), q_weight.astype(jnp.float32), q_bias, w_weight.astype(jnp.float32), w_bias)
    embedding, pullback = jax.vjp(forward, *primals)
    grads = pullback(cotangent.astype(jnp.float32))
    return (embedding, grads[0], grads[1], grads[2], grads[3], grads[4], grads[5])
```

```python
import jax
import jax.numpy as jnp
from jax import lax
from jax.sharding import PartitionSpec as P

F32 = jnp.float32
BF16 = jnp.bfloat16


def contract_rows(left, right):
    return lax.dot_general(
        left, right, (((0,), (0,)), ((), ())), preferred_element_type=jnp.float32
    )


def contract_cols(left, right):
    return lax.dot_general(
        left, right, (((1,), (1,)), ((), ())), preferred_element_type=jnp.float32
    )


def silu_slope(value):
    sigma = jax.nn.sigmoid(value)
    return sigma * (1.0 + value * (1.0 - sigma))


def swap(value, axis, mask):
    size = lax.axis_size(axis)
    return lax.ppermute(value, axis, [(s, s ^ mask) for s in range(size)])


def bit_of(axis, mask):
    return (lax.axis_index(axis) // mask) % 2


def pack_bias(bias):
    high = bias.astype(BF16)
    low = (bias - high.astype(F32)).astype(BF16)
    return jnp.concatenate([high[None], low[None], jnp.zeros((14,) + bias.shape, BF16)], axis=0)


def read_bias(packed):
    return packed[0].astype(F32) + packed[1].astype(F32)


def halve(value, bias, axis, mask):
    half = value.shape[0] // 2
    bit = bit_of(axis, mask)
    keep = lax.dynamic_slice_in_dim(value, bit * half, half)
    send = lax.dynamic_slice_in_dim(value, (1 - bit) * half, half).astype(BF16)
    got = swap(send if bias is None else jnp.concatenate([send, bias], axis=0), axis, mask)
    total = keep + got[:half].astype(F32)
    if bias is None:
        return total, None
    return total, pack_bias(read_bias(bias) + read_bias(got[half:]))


def double(value, axis, mask):
    got = swap(value, axis, mask)
    bit = bit_of(axis, mask)
    return jnp.where(
        bit == 0, jnp.concatenate([value, got], axis=0), jnp.concatenate([got, value], axis=0)
    )


def all_sum(value, bias):
    rows, columns = value.shape
    bias = pack_bias(bias)
    value, bias = halve(value, bias, "rep", 1)
    first, second = jnp.split(value, 2, axis=0)
    first, bias = halve(first, bias, "dom", 1)
    second, _ = halve(second, None, "rep", 2)
    first, bias = halve(first, bias, "rep", 2)
    second, _ = halve(second, None, "dom", 1)
    part = first.shape[0] // 4
    block = jnp.stack(
        [first.reshape(4, part, columns), second.reshape(4, part, columns)], axis=1
    ).reshape(4, 2 * part, columns)
    mine = lax.axis_index("dom") // 2 % 4
    total = lax.dynamic_index_in_dim(block, mine, 0, keepdims=False)
    sums = [read_bias(bias)]
    for step in (1, 2, 3):
        send = lax.dynamic_index_in_dim(block, mine ^ step, 0, keepdims=False).astype(BF16)
        got = swap(jnp.concatenate([send, bias], axis=0), "dom", 2 * step)
        total = total + got[: 2 * part].astype(F32)
        sums.append(read_bias(got[2 * part :]))
    bias_sum = (sums[0] + sums[1]) + (sums[2] + sums[3])
    mask = 8
    while mask < lax.axis_size("dom"):
        total = total.astype(BF16).astype(F32)
        total = total + swap(total, "dom", mask)
        bias_sum = bias_sum + swap(bias_sum, "dom", mask)
        mask *= 2
    total = total.astype(BF16)
    gathered = jnp.zeros((4, 2 * part, columns), BF16)
    gathered = lax.dynamic_update_index_in_dim(gathered, total, mine, 0)
    for step in (1, 2, 3):
        got = swap(total, "dom", 2 * step)
        gathered = lax.dynamic_update_index_in_dim(gathered, got, mine ^ step, 0)
    gathered = gathered.reshape(4, 2, part, columns)
    first = double(gathered[:, 0].reshape(4 * part, columns), "rep", 2)
    second = double(gathered[:, 1].reshape(4 * part, columns), "dom", 1)
    first = double(first, "dom", 1)
    second = double(second, "rep", 2)
    return double(jnp.concatenate([first, second], axis=0), "rep", 1).astype(F32), bias_sum


def build_adjacency(neighbours, importance, columns):
    rows, slots = neighbours.shape
    block = min(256, rows)
    column_ids = lax.iota(jnp.int32, columns)

    def build_one_block(pair):
        index, weight = pair
        match = index[:, :, None] == column_ids[None, None, :]
        return jnp.sum(jnp.where(match, weight[:, :, None], 0.0), axis=1)

    blocks = lax.map(
        build_one_block,
        (
            neighbours.reshape(rows // block, block, slots),
            importance.reshape(rows // block, block, slots),
        ),
    )
    return blocks.reshape(rows, columns)


def send_table(send_rows, rows):
    row_ids = lax.iota(jnp.int32, rows)
    return (send_rows[:, None] == row_ids[None, :]).astype(BF16)


def per_device(
    features,
    node_type,
    neighbours,
    importance,
    send_rows,
    live_rows,
    proj_board,
    q_weight,
    q_bias,
    w_weight,
    w_bias,
    cotangent,
):
    rows = features.shape[0]
    width = q_weight.shape[0]
    board_width = proj_board.shape[0]
    live = (lax.iota(jnp.int32, rows) < live_rows[0])[:, None]
    board = (node_type == 1)[:, None]
    lowered = features[:, :board_width]
    projected = jnp.dot(lowered, proj_board, preferred_element_type=jnp.float32)
    hidden = jnp.where(board, projected, features.astype(jnp.float32)).astype(jnp.bfloat16)
    pre = jnp.dot(hidden, q_weight, preferred_element_type=jnp.float32) + q_bias
    active = jax.nn.silu(pre).astype(jnp.bfloat16)
    onehot = send_table(send_rows, rows)
    outgoing = jnp.dot(onehot, active, preferred_element_type=F32).astype(BF16)
    incoming = lax.all_to_all(outgoing, "dom", split_axis=0, concat_axis=0, tiled=True)
    table = jnp.concatenate([active, incoming], axis=0)
    columns = table.shape[0]
    weights = importance.astype(BF16).astype(F32)
    total = jnp.sum(weights, axis=1, keepdims=True)
    adjacency = build_adjacency(neighbours, weights, columns).astype(BF16)
    agg = jnp.dot(adjacency, table, preferred_element_type=jnp.float32)
    mean = agg / total
    joined = jnp.concatenate([hidden, mean.astype(jnp.bfloat16)], axis=1)
    pre2 = jnp.dot(joined, w_weight, preferred_element_type=jnp.float32) + w_bias
    post = jax.nn.silu(pre2)
    scale = lax.rsqrt(jnp.sum(post * post, axis=1, keepdims=True) + 1e-06)
    embedding = jnp.where(live, post * scale, 0.0)
    grad_out = jnp.where(live, cotangent.astype(jnp.float32), 0.0)
    dpost = scale * grad_out - post * (scale * scale * scale) * jnp.sum(
        post * grad_out, axis=1, keepdims=True
    )
    dpre2 = (dpost * silu_slope(pre2)).astype(jnp.bfloat16)
    grad_w = contract_rows(joined, dpre2)
    grad_w_bias = jnp.sum(dpre2.astype(jnp.float32), axis=0)
    djoined = contract_cols(dpre2, w_weight)
    dagg = (djoined[:, width:] / total).astype(BF16)
    dtable = contract_rows(adjacency, dagg)
    returned = lax.all_to_all(
        dtable[rows:].astype(jnp.bfloat16), "dom", split_axis=0, concat_axis=0, tiled=True
    )
    grad_w, grad_w_bias = all_sum(grad_w, grad_w_bias)
    owned = contract_rows(onehot, returned)
    dactive = dtable[:rows] + owned
    dpre = (dactive * silu_slope(pre)).astype(jnp.bfloat16)
    grad_q = contract_rows(hidden, dpre)
    grad_q_bias = jnp.sum(dpre.astype(jnp.float32), axis=0)
    dhidden = (contract_cols(dpre, q_weight) + djoined[:, :width]).astype(jnp.bfloat16)
    board_part = contract_cols(dhidden, proj_board)
    board_full = jnp.concatenate(
        [board_part, jnp.zeros((rows, width - board_width), jnp.float32)], axis=1
    )
    grad_features = jnp.where(board, board_full, dhidden.astype(jnp.float32))
    grad_proj = contract_rows(lowered, jnp.where(board, dhidden, jnp.zeros_like(dhidden)))
    late, grad_q_bias = all_sum(jnp.concatenate([grad_q, grad_proj], axis=0), grad_q_bias)
    return (embedding, grad_features, late[width:], late[:width], grad_q_bias, grad_w, grad_w_bias)


def solution(mesh):
    placed = (
        P(("dom", "rep"), None),
        P(("dom", "rep")),
        P(("dom", "rep"), None),
        P(("dom", "rep"), None),
        P(("dom", "rep")),
        P(("dom", "rep")),
        P(),
        P(),
        P(),
        P(),
        P(),
        P(("dom", "rep"), None),
    )
    return jax.shard_map(
        per_device,
        mesh=mesh,
        in_specs=placed,
        out_specs=(P(("dom", "rep"), None), P(("dom", "rep"), None), P(), P(), P(), P(), P()),
        check_vma=False,
    )
```

```python
import functools

import jax
import jax.numpy as jnp
from jax import lax
from jax.experimental import pallas as pl
from jax.experimental.pallas import tpu as pltpu
from jax.sharding import PartitionSpec as P

F32 = jnp.float32
BF16 = jnp.bfloat16
LANES = 128
BLOCK = 256
MEGA = 1024 * 1024
ROWS_ROWS = (((0,), (0,)), ((), ()))
COLS_COLS = (((1,), (1,)), ((), ()))
VMEM = pl.BlockSpec(memory_space=pltpu.VMEM)
SMEM = pl.BlockSpec(memory_space=pltpu.SMEM)
ANY = pl.BlockSpec(memory_space=pl.ANY)


COST = pl.CostEstimate(flops=0, bytes_accessed=0, transcendentals=0)


def dot(left, right):
    return jnp.dot(left, right, preferred_element_type=F32)


def contract_rows(left, right):
    return lax.dot_general(left, right, ROWS_ROWS, preferred_element_type=F32)


def contract_cols(left, right):
    return lax.dot_general(left, right, COLS_COLS, preferred_element_type=F32)


def whole(*shape):
    return pl.BlockSpec(shape, lambda *_: (0,) * len(shape), pipeline_mode=pl.Buffered(1))


def shape(dims, dtype):
    return jax.ShapeDtypeStruct(dims, dtype)


def call(kernel, outs, in_specs, out_specs, scratch, tokens=()):
    count, extra = len(in_specs), len(tokens)

    def run(*refs):
        return kernel(*refs[:count], *refs[count + extra :])

    built = pl.pallas_call(
        run,
        out_shape=outs,
        in_specs=list(in_specs) + [ANY] * extra,
        out_specs=out_specs,
        scratch_shapes=list(scratch),
        compiler_params=pltpu.CompilerParams(vmem_limit_bytes=60 * MEGA),
        cost_estimate=COST,
    )
    return lambda *operands: built(*operands, *tokens)


class Copies:
    def __init__(self, arrived):
        self.arrived = arrived
        self.used = 0

    def start(self, source, target):
        copy = pltpu.make_async_copy(source, target, self.arrived.at[self.used])
        self.used += 1
        copy.start()
        return copy


def blocks(count, size=BLOCK):
    return [slice(first, first + size) for first in range(0, count, size)]


def add_up(low):
    rows, width = low.shape
    return jnp.sum(low.astype(F32).reshape(rows // 8, 8, width), axis=0)


def outgoing_kernel(
    send, board, features_hbm, proj_hbm, q_hbm, q_bias, out, features, proj, q_weight, arrived
):
    copies = Copies(arrived)
    got_features = copies.start(features_hbm, features)
    got_proj = copies.start(proj_hbm, proj)
    got_q = copies.start(q_hbm, q_weight)
    rows, width = features.shape
    lowered = proj.shape[0]
    size = min(512, out.shape[0])
    for step, here in enumerate(blocks(out.shape[0], size)):
        names = jnp.broadcast_to(send[:, here], (LANES, size)).T
        lane = lax.broadcasted_iota(jnp.int32, (size, LANES), 1)
        match = [names == lane + first for first in range(0, rows, LANES)]
        hot = jnp.concatenate([jnp.where(m, 1.0, 0.0) for m in match], axis=1)
        kinds = jnp.sum(hot * board[...].astype(F32), axis=1, keepdims=True)
        if step == 0:
            got_features.wait()
        picked = dot(hot.astype(BF16), features[...])
        if step == 0:
            got_proj.wait()
        projected = dot(picked[:, :lowered].astype(BF16), proj[...])
        left = jnp.where(kinds > 0.5, projected, picked[:, :width]).astype(BF16)
        if step == 0:
            got_q.wait()
        pre = dot(left, q_weight[...]) + q_bias[...]
        out[here] = (pre * jax.nn.sigmoid(pre)).astype(BF16)


def local_kernel(
    names, weights, kinds, q_bias, w_bias, features_hbm, proj_hbm, q_hbm, w_hbm,
    near_hbm, far_hbm, hidden_hbm, slope_hbm, agg_hbm, base_hbm,
    features, proj, q_weight, w_top, near, far, hidden, active, slope, agg, base, arrived,
):
    copies = Copies(arrived)
    rows, width = features.shape
    lowered = proj.shape[0]
    got = [
        copies.start(features_hbm, features),
        copies.start(proj_hbm, proj),
        copies.start(q_hbm, q_weight),
    ]
    got_w = copies.start(w_hbm.at[:width], w_top)
    slots = names.shape[1]
    near_heights = near.shape[1] // LANES
    heights = near_heights + far.shape[1] // LANES

    def eight(group):
        name = names[pl.ds(group, 1), :]
        lane = lax.broadcasted_iota(jnp.int32, (LANES, slots), 0)
        hot = jnp.where(lane == (name & (LANES - 1)), 1.0, 0.0).astype(BF16)
        node = lax.broadcasted_iota(jnp.int32, (1, slots), 1) // (slots // 8)
        key = (name >> 7) * 8 + node
        row = lax.broadcasted_iota(jnp.int32, (8 * heights, slots), 0)
        held = jnp.where(row == key, weights[pl.ds(group, 1), :], 0.0)
        return contract_cols(held.astype(BF16), hot)

    def pair(step, _):
        first, second = eight(2 * step), eight(2 * step + 1)
        place = pl.ds(pl.multiple_of(16 * step, 16), 16)
        for h in range(heights):
            both = jnp.concatenate([first[8 * h : 8 * h + 8], second[8 * h : 8 * h + 8]], axis=0)
            if h < near_heights:
                near[place, h * LANES : (h + 1) * LANES] = both.astype(BF16)
            else:
                at = h - near_heights
                far[place, at * LANES : (at + 1) * LANES] = both.astype(BF16)
        return 0

    lax.fori_loop(0, names.shape[0] // 2, pair, 0, unroll=4)
    out = [copies.start(near, near_hbm), copies.start(far, far_hbm)]
    for copy in got:
        copy.wait()
    for here in blocks(rows):
        own = features[here]
        projected = dot(own[:, :lowered], proj[...])
        left = jnp.where(kinds[here] == 1, projected, own.astype(F32)).astype(BF16)
        hidden[here] = left
        pre = dot(left, q_weight[...]) + q_bias[...]
        sigma = jax.nn.sigmoid(pre)
        active[here] = (pre * sigma).astype(BF16)
        slope[here] = sigma * (1.0 + pre * (1.0 - sigma))
    out += [copies.start(hidden, hidden_hbm), copies.start(slope, slope_hbm)]
    got_w.wait()
    for here in blocks(rows):
        agg[here] = dot(near[here], active[...])
        base[here] = dot(hidden[here], w_top[...]) + w_bias[...]
        out += [copies.start(agg.at[here], agg_hbm.at[here])]
        out += [copies.start(base.at[here], base_hbm.at[here])]
    for copy in out:
        copy.wait()


def combine_kernel(
    live, weight, far_hbm, incoming_hbm, agg_hbm, base_hbm, w_hbm, cotangent_hbm,
    embedding_hbm, mean_hbm, dpre2_hbm, dagg_hbm, to_peers_hbm, bias,
    far, incoming, agg, base, w_low, cotangent, embedding, mean, dpre2, dagg, to_peers, arrived,
):
    copies = Copies(arrived)
    rows, width = agg.shape
    parts = blocks(rows)
    got_first = [copies.start(incoming_hbm, incoming), copies.start(far_hbm, far)]
    got_agg = [copies.start(agg_hbm.at[parts[0]], agg.at[parts[0]])]
    got_w = copies.start(w_hbm.at[width:], w_low)
    got_base = [copies.start(base_hbm.at[parts[0]], base.at[parts[0]])]
    got_cotangent = copies.start(cotangent_hbm, cotangent)
    for here in parts[1:]:
        got_agg.append(copies.start(agg_hbm.at[here], agg.at[here]))
        got_base.append(copies.start(base_hbm.at[here], base.at[here]))
    out = []
    total = jnp.zeros(bias.shape, F32)
    for step, here in enumerate(parts):
        if step == 0:
            for copy in got_first:
                copy.wait()
        got_agg[step].wait()
        average = ((agg[here] + dot(far[here], incoming[...])) * weight[here]).astype(BF16)
        mean[here] = average
        if step == 0:
            got_w.wait()
        got_base[step].wait()
        pre = base[here] + dot(average, w_low[...])
        if step == 0:
            got_cotangent.wait()
        sigma = jax.nn.sigmoid(pre)
        post = pre * sigma
        scale = lax.rsqrt(jnp.sum(post * post, axis=1, keepdims=True) + 1e-06)
        row = lax.broadcasted_iota(jnp.int32, (BLOCK, 1), 0) + step * BLOCK
        alive = row < live[0]
        embedding[here] = jnp.where(alive, post * scale, 0.0)
        grad = jnp.where(alive, cotangent[here].astype(F32), 0.0)
        lean = scale * scale * scale * jnp.sum(post * grad, axis=1, keepdims=True)
        dpost = scale * grad - post * lean
        low = (dpost * (sigma * (1.0 + pre * (1.0 - sigma)))).astype(BF16)
        dpre2[here] = low
        total += add_up(low)
        dagg[here] = (contract_cols(low, w_low[...]) * weight[here]).astype(BF16)
        out.append(copies.start(embedding.at[here], embedding_hbm.at[here]))
    bias[...] = total
    out += [copies.start(mean, mean_hbm), copies.start(dpre2, dpre2_hbm)]
    out += [copies.start(dagg, dagg_hbm)]
    for there in blocks(far.shape[1]):
        to_peers[there] = contract_rows(far[:, there], dagg[...]).astype(BF16)
    out += [copies.start(to_peers, to_peers_hbm)]
    for copy in out:
        copy.wait()


def write_pieces(bits, left, right, out, at):
    streams, places, _, columns = out.shape
    piece = left.shape[1] // places
    size = min(BLOCK, left.shape[1])
    for step, here in enumerate(blocks(left.shape[1], size)):
        product = contract_rows(left[:, here], right[...])
        for j in range(size // piece):
            name = step * (size // piece) + j
            rows = product[j * piece : (j + 1) * piece]
            for s in range(streams):
                part = rows[:, s * columns : (s + 1) * columns]
                out[s, name ^ bits[1 + s], at : at + piece] = part.astype(out.dtype)


def start_half(choice, low, high, target, semaphore):
    @pl.when(choice == 0)
    def _():
        pltpu.make_async_copy(low, target, semaphore).start()

    @pl.when(choice == 1)
    def _():
        pltpu.make_async_copy(high, target, semaphore).start()

    return pltpu.make_async_copy(low, target, semaphore)


def w_sent_kernel(bits, hidden_hbm, mean_hbm, dpre2_hbm, out, left, dpre2, arrived):
    got = start_half(1 - bits[0], hidden_hbm, mean_hbm, left, arrived.at[0])
    copy = pltpu.make_async_copy(dpre2_hbm, dpre2, arrived.at[1])
    copy.start()
    got.wait()
    copy.wait()
    write_pieces(bits, left, dpre2, out, 0)


def w_kept_kernel(
    bits, hidden_hbm, mean_hbm, dpre2_hbm, near_hbm, dagg_hbm, w_hbm,
    out_hbm, dtable_hbm, djoined_hbm,
    left, dpre2, near, dagg, w_top, out, dtable, djoined, arrived,
):
    copies = Copies(arrived)
    rows, width = dpre2.shape
    got_dpre2 = copies.start(dpre2_hbm, dpre2)
    copies.used += 1
    got_left = start_half(bits[0], hidden_hbm, mean_hbm, left, arrived.at[copies.used - 1])
    got_w = copies.start(w_hbm.at[:width], w_top)
    got_near = copies.start(near_hbm, near)
    got_dagg = copies.start(dagg_hbm, dagg)
    got_dpre2.wait()
    got_left.wait()
    write_pieces(bits, left, dpre2, out, 0)
    back = [copies.start(out, out_hbm)]
    got_w.wait()
    got_near.wait()
    got_dagg.wait()
    for here in blocks(rows):
        dtable[here] = contract_rows(near[:, here], dagg[...])
        back.append(copies.start(dtable.at[here], dtable_hbm.at[here]))
    for here in blocks(rows):
        djoined[here] = contract_cols(dpre2[here], w_top[...])
        back.append(copies.start(djoined.at[here], djoined_hbm.at[here]))
    for copy in back:
        copy.wait()


def late_sent_kernel(
    bits, send, kinds, returned_hbm, dtable_hbm, slope_hbm, hidden_hbm, q_hbm, djoined_hbm,
    features_hbm, dpre_hbm, dhidden_hbm, dboard_hbm, out, bias,
    returned, dtable, slope, left, q_weight, djoined, features, dpre, dhidden, dboard, arrived,
):
    copies = Copies(arrived)
    rows, width = dtable.shape
    half, lowered = left.shape[1], features.shape[1] * 2
    parts = blocks(rows)
    got_returned = copies.start(returned_hbm, returned)
    got = []
    for here in parts:
        got.append(copies.start(dtable_hbm.at[here], dtable.at[here]))
        got.append(copies.start(slope_hbm.at[here], slope.at[here]))
    copies.used += 2
    got_left = start_half(
        1 - bits[0], hidden_hbm.at[:, :half], hidden_hbm.at[:, half:], left,
        arrived.at[copies.used - 1],
    )
    got_q = copies.start(q_hbm, q_weight)
    got_djoined = copies.start(djoined_hbm, djoined)
    got_features = start_half(
        1 - bits[0], features_hbm.at[:, : lowered // 2], features_hbm.at[:, lowered // 2 : lowered],
        features, arrived.at[copies.used - 4],
    )
    got_returned.wait()
    total = jnp.zeros(bias.shape, F32)
    for step, here in enumerate(parts):
        row = lax.broadcasted_iota(jnp.int32, (BLOCK, send.shape[1]), 0) + step * BLOCK
        hot = jnp.where(row == send[...], 1.0, 0.0).astype(BF16)
        owned = dot(hot, returned[...])
        got[2 * step].wait()
        got[2 * step + 1].wait()
        low = ((dtable[here] + owned) * slope[here]).astype(BF16)
        dpre[here] = low
        total += add_up(low)
    bias[...] = total
    back = [copies.start(dpre, dpre_hbm)]
    got_left.wait()
    write_pieces(bits, left, dpre, out, 0)
    got_q.wait()
    got_djoined.wait()
    for here in parts:
        low = (contract_cols(dpre[here], q_weight[...]) + djoined[here]).astype(BF16)
        dhidden[here] = low
        dboard[here] = jnp.where(kinds[here] == 1, low, jnp.zeros_like(low))
    back += [copies.start(dhidden, dhidden_hbm), copies.start(dboard, dboard_hbm)]
    got_features.wait()
    write_pieces(bits, features, dboard, out, half // 16)
    for copy in back:
        copy.wait()


def late_kept_kernel(
    bits, hidden_hbm, dpre_hbm, features_hbm, dboard_hbm, out,
    left, dpre, features, dboard, arrived,
):
    half, lowered = left.shape[1], features.shape[1] * 2
    got = [
        start_half(bits[0], hidden_hbm.at[:, :half], hidden_hbm.at[:, half:], left, arrived.at[0]),
        start_half(
            bits[0], features_hbm.at[:, : lowered // 2],
            features_hbm.at[:, lowered // 2 : lowered], features, arrived.at[1],
        ),
        pltpu.make_async_copy(dpre_hbm, dpre, arrived.at[2]),
        pltpu.make_async_copy(dboard_hbm, dboard, arrived.at[3]),
    ]
    got[2].start()
    got[3].start()
    got[0].wait()
    got[2].wait()
    write_pieces(bits, left, dpre, out, 0)
    got[1].wait()
    got[3].wait()
    write_pieces(bits, features, dboard, out, half // 16)


def grad_features_kernel(dhidden, dboard, kinds, proj, out):
    lowered = proj.shape[0]
    part = contract_cols(dboard[...], proj[...])
    is_board = kinds[...] == 1
    own = dhidden[...].astype(F32)
    out[:, :lowered] = jnp.where(is_board, part, own[:, :lowered])
    out[:, lowered:] = jnp.where(is_board, 0.0, own[:, lowered:])


def ordered_body(bits, held, *refs, count):
    streams, places, _, columns = held.shape
    outs = refs[-count:]
    for s in range(streams):
        for name in range(places):
            place = name ^ bits[1 + s]
            first = 0
            for out in outs:
                piece = out.shape[0] // places
                block = held[s, place, first : first + piece]
                out[name * piece : (name + 1) * piece, s * columns : (s + 1) * columns] = (
                    block.astype(F32)
                )
                first += piece


def ordered(bits, held, sizes, other, into=None):
    columns = held.shape[3] * 2
    halves = [16 * size for size in sizes]
    side = (lambda i, b: (1 - b[0], 0)) if other else (lambda i, b: (b[0], 0))
    kernel = functools.partial(ordered_body, count=len(sizes))
    operands = [bits, held] + list(into or ())
    return pl.pallas_call(
        kernel,
        out_shape=[shape((2 * half, columns), F32) for half in halves],
        grid_spec=pltpu.PrefetchScalarGridSpec(
            num_scalar_prefetch=1,
            grid=(1,),
            in_specs=[whole(*held.shape)] + [ANY] * len(into or ()),
            out_specs=[pl.BlockSpec((half, columns), side) for half in halves],
        ),
        input_output_aliases={2 + i: i for i in range(len(into or ()))},
        compiler_params=pltpu.CompilerParams(vmem_limit_bytes=60 * MEGA),
        cost_estimate=COST,
    )(*operands)


def swap(value, axis, mask):
    size = lax.axis_size(axis)
    return lax.ppermute(value, axis, [(s, s ^ mask) for s in range(size)])


def sum_pieces(sent, kept):
    piece, columns = kept.shape[2:]
    got = swap(sent, "rep", 1)
    dims = (2, 2, 2, 4, piece, columns)
    got = got.reshape(dims)
    kept = kept.reshape(dims)
    ways = (("dom", 1), ("rep", 2))
    streams = []
    for s in (0, 1):
        away = (kept[s, 1] + got[s, 1].astype(F32)).astype(BF16)
        back = swap(away, *ways[s])
        streams.append(kept[s, 0] + got[s, 0].astype(F32) + back.astype(F32))
    for s in (0, 1):
        back = swap(streams[s][1].astype(BF16), *ways[1 - s])
        streams[s] = streams[s][0] + back.astype(F32)
    block = jnp.stack(streams, axis=1)
    total = block[0]
    for step in (1, 2, 3):
        total = total + swap(block[step].astype(BF16), "dom", 2 * step).astype(F32)
    mask = 8
    while mask < lax.axis_size("dom"):
        low = total.astype(BF16)
        total = low.astype(F32) + swap(low, "dom", mask).astype(F32)
        mask *= 2
    total = total.astype(BF16)
    spread = jnp.stack([total] + [swap(total, "dom", 2 * step) for step in (1, 2, 3)], axis=1)
    streams = [spread[0], spread[1]]
    for s in (0, 1):
        streams[s] = jnp.stack([streams[s], swap(streams[s], *ways[1 - s])])
    for s in (0, 1):
        streams[s] = jnp.stack([streams[s], swap(streams[s], *ways[s])])
    mine = jnp.stack(streams).reshape(2, 16, piece, columns)
    return mine, swap(mine, "rep", 1)


def sum_biases(parts):
    for axis in ("rep", "dom"):
        mask = 1
        while mask < lax.axis_size(axis):
            parts = parts + swap(parts, axis, mask)
            mask *= 2
    return parts


def per_device(
    features,
    node_type,
    neighbours,
    importance,
    send_rows,
    live_rows,
    proj_board,
    q_weight,
    q_bias,
    w_weight,
    w_bias,
    cotangent,
):
    rows, width = features.shape
    lowered = proj_board.shape[0]
    halo = send_rows.shape[0]
    slots = importance.shape[1]
    dom = lax.axis_index("dom")
    rep = lax.axis_index("rep")
    core, y, x, z = rep % 2, rep // 2 % 2, dom % 2, dom // 2 % 4
    bits = jnp.stack([core, x * 8 + y * 4 + z, y * 8 + x * 4 + z]).astype(jnp.int32)
    send_row = send_rows.reshape(1, halo)
    board_row = node_type.reshape(1, rows)
    kinds = node_type.reshape(rows, 1)
    q_bias_row = q_bias.reshape(1, width)
    w_bias_row = w_bias.reshape(1, width)
    low = (rows, width)
    half, quarter = width // 2, lowered // 2

    def buffers(*dims):
        return [pltpu.VMEM(d, kind) for d, kind in dims]

    def semaphores(count):
        return [pltpu.SemaphoreType.DMA((count,))]

    outgoing = call(
        outgoing_kernel,
        shape((halo, width), BF16),
        [whole(1, halo), whole(1, rows), ANY, ANY, ANY, whole(1, width)],
        whole(halo, width),
        buffers((low, BF16), ((lowered, width), BF16), ((width, width), BF16)) + semaphores(3),
    )(send_row, board_row, features, proj_board, q_weight, q_bias_row)
    incoming = lax.all_to_all(outgoing, "dom", split_axis=0, concat_axis=0, tiled=True)

    wide = -(-slots // 64) * 64
    pad = ((0, 0), (0, wide - slots))
    names = jnp.pad(neighbours, pad, constant_values=-1).reshape(rows // 8, 8 * wide)
    weights = jnp.pad(importance, pad).reshape(rows // 8, 8 * wide)
    near, far, hidden, slope, agg, base = call(
        local_kernel,
        (shape((rows, rows), BF16), shape((rows, halo), BF16), shape(low, BF16))
        + (shape(low, F32),) * 3,
        [whole(rows // 8, 8 * wide)] * 2 + [whole(rows, 1)] + [whole(1, width)] * 2 + [ANY] * 4,
        (ANY,) * 6,
        buffers((low, BF16), ((lowered, width), BF16), ((width, width), BF16))
        + buffers(((width, width), BF16), ((rows, rows), BF16), ((rows, halo), BF16))
        + buffers((low, BF16), (low, BF16), (low, F32), (low, F32), (low, F32))
        + semaphores(8 + 2 * (rows // BLOCK)),
        tokens=(outgoing,),
    )(names, weights, kinds, q_bias_row, w_bias_row, features, proj_board, q_weight, w_weight)

    weight = (1.0 / jnp.sum(importance, axis=1)).reshape(rows, 1)
    embedding, mean, dpre2, dagg, to_peers, w_bias_part = call(
        combine_kernel,
        (shape(low, F32), shape(low, BF16), shape(low, BF16), shape(low, BF16))
        + (shape((halo, width), BF16), shape((8, width), F32)),
        [SMEM, whole(rows, 1)] + [ANY] * 6,
        (ANY,) * 5 + (whole(8, width),),
        buffers(((rows, halo), BF16), ((halo, width), BF16), (low, F32), (low, F32))
        + buffers(((width, width), BF16), (low, BF16), (low, F32), (low, BF16), (low, BF16))
        + buffers((low, BF16), ((halo, width), BF16))
        + semaphores(8 + 3 * (rows // BLOCK)),
    )(live_rows, weight, far, incoming, agg, base, w_weight, cotangent)
    returned = lax.all_to_all(to_peers, "dom", split_axis=0, concat_axis=0, tiled=True)

    w_dims = (2, 16, width // 16, half)
    w_sent = call(
        w_sent_kernel,
        shape(w_dims, BF16),
        [SMEM] + [ANY] * 3,
        whole(*w_dims),
        buffers((low, BF16), (low, BF16)) + semaphores(2),
        tokens=(to_peers,),
    )(bits, hidden, mean, dpre2)
    w_kept, dtable, djoined = call(
        w_kept_kernel,
        (shape(w_dims, F32), shape(low, F32), shape(low, F32)),
        [SMEM] + [ANY] * 6,
        (ANY,) * 3,
        buffers((low, BF16), (low, BF16), ((rows, rows), BF16), (low, BF16))
        + buffers(((width, width), BF16), (w_dims, F32), (low, F32), (low, F32))
        + semaphores(6 + 2 * (rows // BLOCK)),
        tokens=(w_sent,),
    )(bits, hidden, mean, dpre2, near, dagg, w_weight)
    w_mine, w_other = sum_pieces(w_sent, w_kept)

    piece = (width + lowered) // 32
    late_dims = (2, 16, piece, half)
    dpre, dhidden, dboard, late_sent, q_bias_part = call(
        late_sent_kernel,
        (shape(low, BF16),) * 3 + (shape(late_dims, BF16), shape((8, width), F32)),
        [SMEM, whole(1, halo), whole(rows, 1)] + [ANY] * 7,
        (ANY,) * 3 + (whole(*late_dims), whole(8, width)),
        buffers(((halo, width), BF16), (low, F32), (low, F32), ((rows, half), BF16))
        + buffers(((width, width), BF16), (low, F32), ((rows, quarter), BF16))
        + buffers((low, BF16), (low, BF16), (low, BF16))
        + semaphores(8 + 2 * (rows // BLOCK)),
    )(bits, send_row, kinds, returned, dtable, slope, hidden, q_weight, djoined, features)
    late_kept = call(
        late_kept_kernel,
        shape(late_dims, F32),
        [SMEM] + [ANY] * 4,
        whole(*late_dims),
        buffers(((rows, half), BF16), (low, BF16), ((rows, quarter), BF16), (low, BF16))
        + semaphores(4),
        tokens=(late_sent,),
    )(bits, hidden, dpre, features, dboard)
    late_mine, late_other = sum_pieces(late_sent, late_kept)
    grad_features = pl.pallas_call(
        grad_features_kernel,
        out_shape=shape(low, F32),
        grid=(rows // BLOCK,),
        in_specs=[
            pl.BlockSpec((BLOCK, width), lambda i: (i, 0)),
            pl.BlockSpec((BLOCK, width), lambda i: (i, 0)),
            pl.BlockSpec((BLOCK, 1), lambda i: (i, 0)),
            whole(lowered, width),
        ],
        out_specs=pl.BlockSpec((BLOCK, width), lambda i: (i, 0)),
        compiler_params=pltpu.CompilerParams(vmem_limit_bytes=60 * MEGA),
        cost_estimate=COST,
    )(dhidden, dboard, kinds, proj_board)
    parts = jnp.stack([jnp.sum(q_bias_part, axis=0), jnp.sum(w_bias_part, axis=0)])
    biases = sum_biases(parts)
    grad_w = ordered(bits, w_mine, [width // 16], False)
    (grad_w,) = ordered(bits, w_other, [width // 16], True, grad_w)
    late = ordered(bits, late_mine, [width // 32, lowered // 32], False)
    grad_q, grad_proj = ordered(bits, late_other, [width // 32, lowered // 32], True, late)
    return (embedding, grad_features, grad_proj, grad_q, biases[0], grad_w, biases[1])


def solution(mesh):
    placed = (
        P(("dom", "rep"), None),
        P(("dom", "rep")),
        P(("dom", "rep"), None),
        P(("dom", "rep"), None),
        P(("dom", "rep")),
        P(("dom", "rep")),
        P(),
        P(),
        P(),
        P(),
        P(),
        P(("dom", "rep"), None),
    )
    return jax.shard_map(
        per_device,
        mesh=mesh,
        in_specs=placed,
        out_specs=(P(("dom", "rep"), None), P(("dom", "rep"), None), P(), P(), P(), P(), P()),
        check_vma=False,
    )
```

```python
import functools

import jax
import jax.numpy as jnp
from jax import lax
from jax.experimental import pallas as pl
from jax.experimental.pallas import tpu as pltpu
from jax.sharding import PartitionSpec as P

F32 = jnp.float32
BF16 = jnp.bfloat16
LANES = 128
BLOCK = 256
MEGA = 1024 * 1024
MARK = 64.0
PLACES = 16
BIAS_ROWS = 16
ROWS_ROWS = (((0,), (0,)), ((), ()))
COLS_COLS = (((1,), (1,)), ((), ()))
VMEM = pl.BlockSpec(memory_space=pltpu.VMEM)
SMEM = pl.BlockSpec(memory_space=pltpu.SMEM)
ANY = pl.BlockSpec(memory_space=pl.ANY)


COST = pl.CostEstimate(flops=0, bytes_accessed=0, transcendentals=0)


def dot(left, right):
    return jnp.dot(left, right, preferred_element_type=F32)


def contract_rows(left, right):
    return lax.dot_general(left, right, ROWS_ROWS, preferred_element_type=F32)


def contract_cols(left, right):
    return lax.dot_general(left, right, COLS_COLS, preferred_element_type=F32)


def whole(*shape):
    return pl.BlockSpec(shape, lambda *_: (0,) * len(shape), pipeline_mode=pl.Buffered(1))


def shape(dims, dtype):
    return jax.ShapeDtypeStruct(dims, dtype)


def call(kernel, outs, in_specs, out_specs, scratch, tokens=(), moved=0, **more):
    count, extra = len(in_specs), len(tokens)

    def run(*refs):
        return kernel(*refs[:count], *refs[count + extra :])

    built = pl.pallas_call(
        run,
        out_shape=outs,
        in_specs=list(in_specs) + [ANY] * extra,
        out_specs=out_specs,
        scratch_shapes=list(scratch),
        compiler_params=pltpu.CompilerParams(vmem_limit_bytes=60 * MEGA),
        cost_estimate=pl.CostEstimate(flops=0, bytes_accessed=moved * MEGA, transcendentals=0),
    )
    return lambda *operands: built(*operands, *tokens)


class Copies:
    def __init__(self, arrived):
        self.arrived = arrived
        self.used = 0

    def start(self, source, target):
        copy = pltpu.make_async_copy(source, target, self.arrived.at[self.used])
        self.used += 1
        copy.start()
        return copy

    def by_blocks(self, source, target, start=True):
        first, count = self.used, source.shape[0] // BLOCK
        self.used += count

        def block(step):
            here = rows_of(step)
            return pltpu.make_async_copy(
                source.at[here], target.at[here], self.arrived.at[first + step]
            )

        if start:
            each_block(count, lambda step: block(step).start())
        return block


def rows_of(step):
    return pl.ds(pl.multiple_of(step * BLOCK, BLOCK), BLOCK)


def each_block(count, body):
    def run(step, _):
        body(step)
        return 0

    lax.fori_loop(0, count, run, 0)


def sigmoid(value):
    return 0.5 * jnp.tanh(0.5 * value) + 0.5


def add_up(low):
    rows, width = low.shape
    return jnp.sum(low.astype(F32).reshape(rows // 8, 8, width), axis=0)


def outgoing_kernel(send, board, features_hbm, out, features, arrived):
    got = pltpu.make_async_copy(features_hbm, features, arrived.at[0])
    got.start()
    rows, width = features.shape
    size = min(512, out.shape[0])
    for step in range(out.shape[0] // size):
        here = slice(step * size, step * size + size)
        names = jnp.broadcast_to(send[:, here], (LANES, size)).T
        lane = lax.broadcasted_iota(jnp.int32, (size, LANES), 1)
        match = [names == lane + first for first in range(0, rows, LANES)]
        hot = jnp.concatenate([jnp.where(m, 1.0, 0.0) for m in match], axis=1)
        kinds = jnp.sum(hot * board[...].astype(F32), axis=1, keepdims=True)
        if step == 0:
            got.wait()
        picked = dot(hot.astype(BF16), features[...])
        last = width - LANES
        out[here, :last] = picked[:, :last].astype(BF16)
        marked = (kinds > 0.5) & (lane == LANES - 1)
        out[here, last:] = jnp.where(marked, MARK, picked[:, last:]).astype(BF16)


def local_kernel(
    names, weights, kinds, q_bias, w_bias, features_hbm, proj_hbm, q_hbm, w_hbm,
    near_hbm, far_hbm, hidden_hbm, slope_hbm, agg_hbm, base_hbm, lowered_hbm, boards,
    features, proj, q_weight, w_top, near, far, hidden, active, slope, agg, base, masked, arrived,
):
    copies = Copies(arrived)
    rows, width = features.shape
    lowered = proj.shape[0]
    got = [
        copies.start(features_hbm, features),
        copies.start(proj_hbm, proj),
        copies.start(q_hbm, q_weight),
    ]
    got_w = copies.start(w_hbm.at[:width], w_top)
    slots = names.shape[1]
    near_heights = near.shape[1] // LANES
    heights = near_heights + far.shape[1] // LANES

    def eight(group):
        name = names[pl.ds(group, 1), :]
        lane = lax.broadcasted_iota(jnp.int32, (LANES, slots), 0)
        hot = jnp.where(lane == (name & (LANES - 1)), 1.0, 0.0).astype(BF16)
        node = lax.broadcasted_iota(jnp.int32, (1, slots), 1) // (slots // 8)
        key = (name >> 7) * 8 + node
        row = lax.broadcasted_iota(jnp.int32, (8 * heights, slots), 0)
        held = jnp.where(row == key, weights[pl.ds(group, 1), :], 0.0)
        return contract_cols(held.astype(BF16), hot)

    def pair(step, _):
        first, second = eight(2 * step), eight(2 * step + 1)
        place = pl.ds(pl.multiple_of(16 * step, 16), 16)
        for h in range(heights):
            both = jnp.concatenate([first[8 * h : 8 * h + 8], second[8 * h : 8 * h + 8]], axis=0)
            if h < near_heights:
                near[place, h * LANES : (h + 1) * LANES] = both.astype(BF16)
            else:
                at = h - near_heights
                far[place, at * LANES : (at + 1) * LANES] = both.astype(BF16)
        return 0

    lax.fori_loop(0, names.shape[0] // 2, pair, 0, unroll=4)
    out = [copies.start(near, near_hbm), copies.start(far, far_hbm)]
    for copy in got:
        copy.wait()
    count = rows // BLOCK

    def front(step):
        here = rows_of(step)
        own = features[here]
        low = own[:, :lowered]
        is_board = kinds[here] == 1
        boards[here] = jnp.where(is_board, jnp.ones((BLOCK, LANES), F32), 0.0)
        masked[here] = jnp.where(is_board, low, jnp.zeros_like(low))
        left = jnp.where(is_board, dot(low, proj[...]), own.astype(F32)).astype(BF16)
        hidden[here] = left
        pre = dot(left, q_weight[...]) + q_bias[...]
        sigma = sigmoid(pre)
        active[here] = (pre * sigma).astype(BF16)
        slope[here] = sigma + pre * sigma * (1.0 - sigma)

    each_block(count, front)
    out += [copies.start(hidden, hidden_hbm), copies.start(slope, slope_hbm)]
    out += [copies.start(masked, lowered_hbm)]
    got_w.wait()
    agg_out = copies.by_blocks(agg, agg_hbm, start=False)
    base_out = copies.by_blocks(base, base_hbm, start=False)

    def local(step):
        here = rows_of(step)
        agg[here] = dot(near[here], active[...])
        agg_out(step).start()
        base[here] = dot(hidden[here], w_top[...]) + w_bias[...]
        base_out(step).start()

    each_block(count, local)
    for copy in out:
        copy.wait()
    each_block(count, lambda step: agg_out(step).wait())
    each_block(count, lambda step: base_out(step).wait())


def combine_kernel(
    live, bits, weight, q_bias, far_hbm, incoming_hbm, proj_hbm, q_hbm, agg_hbm, base_hbm, w_hbm,
    cotangent_hbm, hidden_hbm,
    embedding_hbm, dpre2_hbm, dagg_hbm, to_peers_hbm, w_sent_hbm, w_kept_hbm, far_hidden_hbm,
    far_dpre_hbm, far_lowered_hbm, far_slope_hbm, bias,
    far, incoming, proj, q_weight, agg, base, w_low, cotangent, hidden, mean, dpre2, dagg, to_peers,
    w_sent, w_kept, far_hidden, far_slope, far_lowered, arrived,
):
    copies = Copies(arrived)
    rows, width = agg.shape
    count = rows // BLOCK
    got_front = [copies.start(incoming_hbm, incoming), copies.start(proj_hbm, proj)]
    got_front += [copies.start(q_hbm, q_weight)]
    got = [copies.start(far_hbm, far), copies.start(w_hbm.at[width:], w_low)]
    got_agg = copies.by_blocks(agg_hbm, agg)
    got_base = copies.by_blocks(base_hbm, base)
    got_cotangent = copies.by_blocks(cotangent_hbm, cotangent)
    got_hidden = copies.start(hidden_hbm, hidden)
    embedding = agg
    embedding_out = copies.by_blocks(embedding, embedding_hbm, start=False)
    dpre2_out = copies.by_blocks(dpre2, dpre2_hbm, start=False)
    dagg_out = copies.by_blocks(dagg, dagg_hbm, start=False)
    outs = [embedding_out, dpre2_out, dagg_out]
    bias[...] = jnp.zeros(bias.shape, F32)
    for copy in got_front:
        copy.wait()
    lowered = proj.shape[0]
    active = incoming
    held = far_hidden.shape[0] == far.shape[1]

    def move(*pairs):
        for i, (source, target) in enumerate(pairs):
            copy = pltpu.make_async_copy(source, target, arrived.at[arrived.shape[0] - 1 - i])
            copy.start()
            copy.wait()

    def front(step):
        here = rows_of(step)
        spot = here if held else pl.ds(0, BLOCK)
        own = incoming[here]
        is_board = own[:, width - 1 :].astype(F32) > MARK / 2
        low = own[:, :lowered]
        far_lowered[spot] = jnp.where(is_board, low, jnp.zeros_like(low))
        left = jnp.where(is_board, dot(low, proj[...]), own.astype(F32)).astype(BF16)
        far_hidden[spot] = left
        pre = dot(left, q_weight[...]) + q_bias[...]
        sigma = sigmoid(pre)
        active[here] = (pre * sigma).astype(BF16)
        far_slope[spot] = sigma + pre * sigma * (1.0 - sigma)
        if not held:
            move(
                (far_lowered, far_lowered_hbm.at[here]),
                (far_hidden, far_hidden_hbm.at[here]),
                (far_slope, far_slope_hbm.at[here]),
            )

    each_block(far.shape[1] // BLOCK, front)
    far_out = []
    if held:
        far_out += [copies.start(far_hidden, far_hidden_hbm)]
        far_out += [copies.start(far_lowered, far_lowered_hbm)]
    for copy in got:
        copy.wait()

    def node_block(step):
        here = rows_of(step)
        got_agg(step).wait()
        average = ((agg[here] + dot(far[here], active[...])) * weight[here]).astype(BF16)
        mean[here] = average
        got_base(step).wait()
        pre = base[here] + dot(average, w_low[...])
        got_cotangent(step).wait()
        sigma = sigmoid(pre)
        post = pre * sigma
        scale = lax.rsqrt(jnp.sum(post * post, axis=1, keepdims=True) + 1e-06)
        row = lax.broadcasted_iota(jnp.int32, (BLOCK, 1), 0) + step * BLOCK
        scale = jnp.where(row < live[0], scale, 0.0)
        embedding[here] = post * scale
        grad = cotangent[here].astype(F32)
        lean = scale * scale * scale * jnp.sum(post * grad, axis=1, keepdims=True)
        dpost = scale * grad - post * lean
        low = (dpost * (sigma + post * (1.0 - sigma))).astype(BF16)
        dpre2[here] = low
        bias[...] += add_up(low)
        dagg[here] = (contract_cols(low, w_low[...]) * weight[here]).astype(BF16)
        for out in outs:
            out(step).start()

    each_block(count, node_block)
    got_hidden.wait()

    stride = width // PLACES

    @pl.when(bits[0] == 1)
    def _():
        write_pieces(bits[2], [(hidden, 0, dpre2)], width, w_sent, stride, 0)
        write_pieces(bits[1], [(mean, 0, dpre2)], width, w_kept, stride, 0)

    @pl.when(bits[0] == 0)
    def _():
        write_pieces(bits[2], [(mean, 0, dpre2)], width, w_sent, stride, 0)
        write_pieces(bits[1], [(hidden, 0, dpre2)], width, w_kept, stride, 0)

    far_out += [copies.start(w_sent, w_sent_hbm), copies.start(w_kept, w_kept_hbm)]
    far_dpre = far_hidden
    if held:
        far_out.pop(0).wait()

    def peer_block(step):
        here = rows_of(step)
        spot = here if held else pl.ds(0, BLOCK)
        if not held:
            move((far_slope_hbm.at[here], far_slope))
        table = contract_rows(far[:, here], dagg[...])
        to_peers[spot] = table.astype(BF16)
        far_dpre[spot] = (table * far_slope[spot]).astype(BF16)
        if not held:
            move((to_peers, to_peers_hbm.at[here]), (far_dpre, far_dpre_hbm.at[here]))

    each_block(far.shape[1] // BLOCK, peer_block)
    if held:
        far_out += [copies.start(to_peers, to_peers_hbm), copies.start(far_dpre, far_dpre_hbm)]
    for copy in far_out:
        copy.wait()
    for out in outs:
        each_block(count, lambda step, out=out: out(step).wait())


def write_pieces(mark, pairs, depth, out, stride, at, plus=None):
    piece = depth // PLACES
    size = min(BLOCK, depth)

    def block(step):
        product = 0.0
        for left, first, right in pairs:
            here = pl.ds(pl.multiple_of(first + step * size, size), size)
            product += contract_rows(left[:, here], right[...])
        write_block(mark, product, step * (size // piece), out, stride, at, piece, plus)

    each_block(depth // size, block)


def write_block(mark, product, first, out, stride, at, piece, plus=None):
    for j in range(product.shape[0] // piece):
        place = (first + j) ^ mark
        here = pl.ds(pl.multiple_of(place * stride + at, 16), piece)
        part = product[j * piece : (j + 1) * piece]
        if plus is not None:
            part += plus[here].astype(F32)
        out[here] = part.astype(out.dtype)


def gradients_kernel(
    bits, w_bias, near_hbm, dagg_hbm, slope_hbm, dpre2_hbm, w_hbm, hidden_hbm,
    far_hidden_hbm, far_dpre_hbm, lowered_hbm, far_lowered_hbm, q_hbm,
    dtable_hbm, djoined_hbm, sent_hbm, kept_hbm,
    near, dagg, slope, dpre2, w_top, hidden, far_hidden, far_dpre, lowered, far_lowered,
    q_weight, dtable, djoined, dpre, sent, kept, bias, arrived,
):
    copies = Copies(arrived)
    rows, width = dpre.shape
    depth = lowered.shape[1]
    half = width // 2
    count = rows // BLOCK
    got_table = [copies.start(dagg_hbm, dagg), copies.start(near_hbm, near)]
    got_slope = copies.by_blocks(slope_hbm, slope)
    got_q = [copies.start(hidden_hbm, hidden), copies.start(far_hidden_hbm, far_hidden)]
    got_q += [copies.start(far_dpre_hbm, far_dpre)]
    got_joined = [copies.start(w_hbm.at[:width], w_top), copies.start(dpre2_hbm, dpre2)]
    got_p = [copies.start(lowered_hbm, lowered), copies.start(far_lowered_hbm, far_lowered)]
    got_p += [copies.start(q_hbm, q_weight)]
    bias[...] = jnp.zeros(bias.shape, F32)
    for copy in got_table:
        copy.wait()

    def table_block(step):
        here = rows_of(step)
        table = contract_rows(near[:, here], dagg[...])
        dtable[here] = table.astype(BF16)
        got_slope(step).wait()
        low = (table * slope[here]).astype(BF16)
        dpre[here] = low
        bias[...] += add_up(low)

    each_block(count, table_block)
    out = [copies.start(dtable, dtable_hbm)]
    for copy in got_q:
        copy.wait()

    def far_block(step):
        bias[...] += add_up(far_dpre[rows_of(step)])

    each_block(far_dpre.shape[0] // BLOCK, far_block)
    stride = (half + depth // 2) // PLACES
    sides = ((sent, 1 - bits[0], bits[2]), (kept, bits[0], bits[1]))
    for target, side, mark in sides:
        first = side * half
        pairs = [(hidden, first, dpre), (far_hidden, first, far_dpre)]
        write_pieces(mark, pairs, half, target, stride, 0)
    for copy in got_joined:
        copy.wait()

    def joined_block(step):
        here = rows_of(step)
        djoined[here] = contract_cols(dpre2[here], w_top[...]).astype(BF16)

    each_block(count, joined_block)
    out += [copies.start(djoined, djoined_hbm)]
    for copy in got_p:
        copy.wait()
    for target, side, mark in sides:
        here = pl.ds(pl.multiple_of(side * (depth // 2), depth // 2), depth // 2)
        part = lowered[:, here]
        through = contract_rows(part, dpre[...]) + contract_rows(far_lowered[:, here], far_dpre[...])
        product = contract_cols(through.astype(BF16), q_weight[...])
        product += contract_rows(part, djoined[...])
        write_block(mark, product, 0, target, stride, half // PLACES, depth // 2 // PLACES)
    row = lax.broadcasted_iota(jnp.int32, (BIAS_ROWS, 1), 0)
    block = jnp.zeros((BIAS_ROWS, width), F32)
    for i, part in enumerate((bias, w_bias)):
        total = jnp.sum(part[...], axis=0, keepdims=True)
        high = total.astype(BF16).astype(F32)
        block = jnp.where(row == i, high, jnp.where(row == i + 2, total - high, block))
    sent[sent.shape[0] - BIAS_ROWS :] = block.astype(BF16)
    out += [copies.start(sent, sent_hbm), copies.start(kept, kept_hbm)]
    for copy in out:
        copy.wait()


def grad_features_kernel(
    send, boards, returned_hbm, dtable_hbm, slope_hbm, q_hbm, djoined_hbm, proj_hbm, grad_hbm,
    returned, dtable, slope, q_weight, djoined, proj, arrived,
):
    copies = Copies(arrived)
    rows = dtable.shape[0]
    lowered = proj.shape[0]
    count = rows // BLOCK
    got = [copies.start(returned_hbm, returned), copies.start(dtable_hbm, dtable)]
    got += [copies.start(q_hbm, q_weight)]
    got_slope = copies.by_blocks(slope_hbm, slope)
    got += [copies.start(djoined_hbm, djoined), copies.start(proj_hbm, proj)]
    grad_out = copies.by_blocks(slope, grad_hbm, start=False)
    for copy in got:
        copy.wait()

    def block(step):
        here = rows_of(step)
        row = lax.broadcasted_iota(jnp.int32, (BLOCK, send.shape[1]), 0) + step * BLOCK
        hot = jnp.where(row == send[...], 1.0, 0.0).astype(BF16)
        owned = dtable[here].astype(F32) + dot(hot, returned[...])
        got_slope(step).wait()
        dpre = (owned * slope[here]).astype(BF16)
        low = (contract_cols(dpre, q_weight[...]) + djoined[here].astype(F32)).astype(BF16)
        product = contract_cols(low, proj[...])
        is_board = boards[here, :1] > 0.5
        own = low.astype(F32)
        slope[here, :lowered] = jnp.where(is_board, product, own[:, :lowered])
        slope[here, lowered:] = jnp.where(is_board, 0.0, own[:, lowered:])
        grad_out(step).start()

    each_block(count, block)
    each_block(count, lambda step: grad_out(step).wait())


def ordered_kernel(bits, held, *refs, count, other):
    outs = refs[-count:]
    mark = bits[2 if other else 1] % 4
    stride = held.shape[0] // 4
    first = 0
    for out in outs:
        piece = out.shape[0] // 4
        for j in range(4):
            here = pl.ds(pl.multiple_of((j ^ mark) * stride + first, 16), piece)
            out[j * piece : (j + 1) * piece] = held[here].astype(F32)
        first += piece


def ordered(bits, held, sizes, other, into=None):
    columns = held.shape[1]
    steps = PLACES // 4
    into = list(into or ())
    mark = 2 if other else 1

    def target(i, b):
        return ((1 - b[0] if other else b[0]) * steps + i, 0)

    return pl.pallas_call(
        functools.partial(ordered_kernel, count=len(sizes), other=other),
        out_shape=[shape((2 * PLACES * size, columns), F32) for size in sizes],
        grid_spec=pltpu.PrefetchScalarGridSpec(
            num_scalar_prefetch=1,
            grid=(steps,),
            in_specs=[pl.BlockSpec((4 * sum(sizes), columns), lambda i, b: (i ^ (b[mark] // 4), 0))]
            + [ANY] * len(into),
            out_specs=[pl.BlockSpec((4 * size, columns), target) for size in sizes],
        ),
        input_output_aliases={2 + i: i for i in range(len(into))},
        compiler_params=pltpu.CompilerParams(vmem_limit_bytes=24 * MEGA),
        cost_estimate=pl.CostEstimate(
            flops=0, bytes_accessed=200 * MEGA, transcendentals=0
        ),
    )(bits, held, *into)


def swap(value, axis, mask):
    size = lax.axis_size(axis)
    return lax.ppermute(value, axis, [(s, s ^ mask) for s in range(size)])


WAYS = (
    (("dom", 1), ("rep", 2)),
    (("rep", 2), ("dom", 1)),
    (("dom", 2), ("dom", 4)),
    (("dom", 4), ("dom", 2)),
)
FAR_WAYS = WAYS[3], WAYS[2], (("dom", 6), ("dom", 6))


def cross(value, ways):
    doms, reps = lax.axis_size("dom"), lax.axis_size("rep")
    pairs = []
    for d in range(doms):
        for r in range(reps):
            axis, mask = ways[r % 2]
            to = (d ^ mask, r) if axis == "dom" else (d, r ^ mask)
            pairs.append((d * reps + r, to[0] * reps + to[1]))
    return lax.ppermute(value, ("dom", "rep"), pairs)


class Order:
    def __init__(self):
        self.last = ()

    def __call__(self, step, *operands):
        held, _ = lax.optimization_barrier((operands, self.last))
        result = step(*held)
        self.last = jax.tree.leaves(result)[:1]
        return result


def pack(bias):
    high = lax.reduce_precision(bias, 8, 7)
    rest = jnp.zeros((BIAS_ROWS - 4, bias.shape[1]), F32)
    return jnp.concatenate([high, bias - high, rest]).astype(BF16)


def unpack(rows):
    rows = rows[-BIAS_ROWS:].astype(F32)
    return rows[:2] + rows[2:4]


class PieceSum:
    def __init__(self, sent, with_bias):
        self.got = swap(sent, "rep", 1)
        self.bias = unpack(sent) if with_bias else None
        self.stage = 0

    def first(self, order, kept):
        self.split(order, kept, self.got)

    def reduce(self, order):
        self.stage += 1
        self.split(order, self.held, self.back)

    def split(self, order, held, back):
        half = held.shape[0] // 2

        def step(held, back, bias):
            stay = held[:half].astype(F32) + back[:half].astype(F32)
            away = (held[half:].astype(F32) + back[half : 2 * half].astype(F32)).astype(BF16)
            if bias is not None:
                bias = bias + unpack(back)
                away = jnp.concatenate([away, pack(bias)])
                bias = unpack(away)
            return away, stay, bias

        away, self.held, self.bias = order(step, held, back, self.bias)
        self.back = cross(away, WAYS[self.stage])

    def reduce_far(self, order):
        part = self.held.shape[0] // 4

        def step(held, back, bias):
            stay = held[:part] + back[:part].astype(F32)
            if bias is not None:
                bias = bias + unpack(back)
                packed = pack(bias)
                bias = unpack(packed)
            aways = []
            for i in (1, 2, 3):
                here = slice(i * part, (i + 1) * part)
                away = (held[here] + back[here].astype(F32)).astype(BF16)
                aways.append(away if bias is None else jnp.concatenate([away, packed]))
            return aways, stay, bias

        aways, self.held, self.bias = order(step, self.held, self.back, self.bias)
        self.back = [cross(away, way) for away, way in zip(aways, FAR_WAYS)]

    def turn_far(self, order):
        rows = self.held.shape[0]

        def step(held, back, bias):
            total = held + sum(b[:rows].astype(F32) for b in back)
            if bias is not None:
                got = [unpack(b) for b in back]
                bias = (bias + got[0]) + (got[1] + got[2])
            return total.astype(BF16), bias

        total, self.bias = order(step, self.held, self.back, self.bias)
        self.held = self.beyond(total)
        self.back = [cross(self.held, way) for way in FAR_WAYS]

    def gather_far(self, order):
        self.held = order(lambda h, b: jnp.concatenate([h] + list(b)), self.held, self.back)
        self.back = cross(self.held, WAYS[self.stage])

    def beyond(self, total):
        mask = 8
        while mask < lax.axis_size("dom"):
            total = (total.astype(F32) + swap(total, "dom", mask).astype(F32)).astype(BF16)
            if self.bias is not None:
                self.bias = self.bias + swap(self.bias, "dom", mask)
            mask *= 2
        return total

    def turn(self, order):
        rows = self.held.shape[0]

        def step(held, back, bias):
            total = (held + back[:rows].astype(F32)).astype(BF16)
            return total, None if bias is None else bias + unpack(back)

        total, self.bias = order(step, self.held, self.back, self.bias)
        self.held = self.beyond(total)
        self.back = cross(self.held, WAYS[self.stage])

    def gather(self, order):
        self.held = order(lambda *parts: jnp.concatenate(parts), self.held, self.back)
        self.stage -= 1
        self.back = cross(self.held, WAYS[self.stage])

    def last(self, order):
        extra = [] if self.bias is None else [pack(self.bias)]
        self.mine = order(lambda *parts: jnp.concatenate(parts), self.held, self.back, *extra)
        self.other = swap(self.mine, "rep", 1)


def per_device(
    features,
    node_type,
    neighbours,
    importance,
    send_rows,
    live_rows,
    proj_board,
    q_weight,
    q_bias,
    w_weight,
    w_bias,
    cotangent,
):
    rows, width = features.shape
    lowered = proj_board.shape[0]
    halo = send_rows.shape[0]
    slots = importance.shape[1]
    dom = lax.axis_index("dom")
    rep = lax.axis_index("rep")
    core, y, x, z = rep % 2, rep // 2 % 2, dom % 2, dom // 2 % 4
    low_z, high_z = z % 2, z // 2
    marks = x * 8 + y * 4 + low_z * 2 + high_z, y * 8 + x * 4 + high_z * 2 + low_z
    own, sibling = jnp.where(core == 0, marks[0], marks[1]), jnp.where(core == 0, marks[1], marks[0])
    bits = jnp.stack([core, own, sibling]).astype(jnp.int32)
    send_row = send_rows.reshape(1, halo)
    board_row = node_type.reshape(1, rows)
    kinds = node_type.reshape(rows, 1)
    q_bias_row = q_bias.reshape(1, width)
    w_bias_row = w_bias.reshape(1, width)
    low = (rows, width)
    half = width // 2

    def buffers(*dims):
        return [pltpu.VMEM(d, kind) for d, kind in dims]

    def semaphores(count):
        return [pltpu.SemaphoreType.DMA((count,))]

    outgoing = call(
        outgoing_kernel,
        shape((halo, width), BF16),
        [whole(1, halo), whole(1, rows), ANY],
        whole(halo, width),
        buffers((low, BF16)) + semaphores(1),
    )(send_row, board_row, features)
    incoming = lax.all_to_all(outgoing, "dom", split_axis=0, concat_axis=0, tiled=True)

    wide = -(-slots // 64) * 64
    pad = ((0, 0), (0, wide - slots))
    names = jnp.pad(neighbours, pad, constant_values=-1).reshape(rows // 8, 8 * wide)
    weights = jnp.pad(importance, pad).reshape(rows // 8, 8 * wide)
    narrow = (rows, lowered)
    near, far, hidden, slope, agg, base, own_lowered, boards = call(
        local_kernel,
        (shape((rows, rows), BF16), shape((rows, halo), BF16), shape(low, BF16))
        + (shape(low, F32),) * 3
        + (shape(narrow, BF16), shape((rows, LANES), F32)),
        [whole(rows // 8, 8 * wide)] * 2 + [whole(rows, 1)] + [whole(1, width)] * 2 + [ANY] * 4,
        (ANY,) * 7 + (whole(rows, LANES),),
        buffers((low, BF16), ((lowered, width), BF16), ((width, width), BF16))
        + buffers(((width, width), BF16), ((rows, rows), BF16), ((rows, halo), BF16))
        + buffers((low, BF16), (low, BF16), (low, F32), (low, F32), (low, F32), (narrow, BF16))
        + semaphores(9 + 2 * (rows // BLOCK)),
        tokens=(outgoing,),
    )(names, weights, kinds, q_bias_row, w_bias_row, features, proj_board, q_weight, w_weight)

    weight = (1.0 / jnp.sum(importance, axis=1)).reshape(rows, 1)
    w_dims = (width, width)
    far_low, far_narrow = (halo, width), (halo, lowered)
    spot = halo if halo <= rows else BLOCK
    (
        embedding, dpre2, dagg, to_peers, w_sent, w_kept, far_hidden, far_dpre, far_lowered, _,
        w_bias_part,
    ) = call(
        combine_kernel,
        (shape(low, F32), shape(low, BF16), shape(low, BF16))
        + (shape(far_low, BF16), shape(w_dims, BF16), shape(w_dims, BF16))
        + (shape(far_low, BF16), shape(far_low, BF16), shape(far_narrow, BF16))
        + (shape(far_low if spot < halo else (8, LANES), F32), shape((8, width), F32)),
        [SMEM, SMEM, whole(rows, 1), whole(1, width)] + [ANY] * 9,
        (ANY,) * 10 + (whole(8, width),),
        buffers(((rows, halo), BF16), (far_low, BF16), ((lowered, width), BF16))
        + buffers(((width, width), BF16), (low, F32), (low, F32), ((width, width), BF16))
        + buffers((low, BF16), (low, BF16), (low, BF16), (low, BF16), (low, BF16))
        + buffers(((spot, width), BF16), (w_dims, BF16), (w_dims, BF16), ((spot, width), BF16))
        + buffers(((spot, width), F32), ((spot, lowered), BF16))
        + semaphores(15 + 6 * (rows // BLOCK)),
    )(
        live_rows, bits, weight, q_bias_row, far, incoming, proj_board, q_weight, agg, base, w_weight,
        cotangent, hidden,
    )
    returned = lax.all_to_all(to_peers, "dom", split_axis=0, concat_axis=0, tiled=True)

    order = Order()
    w_sum = PieceSum(w_sent, False)
    late_rows = (width + lowered) // 2
    sent_dims, kept_dims = (late_rows + BIAS_ROWS, width), (late_rows, width)
    w_sum.first(order, w_kept)
    dtable, djoined, late_sent, late_kept = order(
        call(
            gradients_kernel,
            (shape(low, BF16), shape(low, BF16))
            + (shape(sent_dims, BF16), shape(kept_dims, BF16)),
            [SMEM, whole(8, width)] + [ANY] * 11,
            (ANY,) * 4,
            buffers(((rows, rows), BF16), (low, BF16), (low, F32), (low, BF16))
            + buffers(((width, width), BF16), (low, BF16), (far_low, BF16))
            + buffers((far_low, BF16), (narrow, BF16), (far_narrow, BF16), ((width, width), BF16))
            + buffers((low, BF16), (low, BF16), (low, BF16), (sent_dims, BF16))
            + buffers((kept_dims, BF16), ((8, width), F32))
            + semaphores(16 + rows // BLOCK),
            moved=200,
        ),
        bits, w_bias_part, near, dagg, slope, dpre2, w_weight, hidden, far_hidden, far_dpre,
        own_lowered, far_lowered, q_weight,
    )
    w_sum.reduce(order)
    late_sum = PieceSum(order(lambda sent: sent, late_sent), True)
    returned = order(lambda value: value, returned)
    late_sum.first(order, late_kept)
    grad_features = order(
        call(
            grad_features_kernel,
            shape(low, F32),
            [whole(1, halo), whole(rows, LANES)] + [ANY] * 6,
            ANY,
            buffers((far_low, BF16), (low, BF16), (low, F32), ((width, width), BF16))
            + buffers((low, BF16), ((lowered, width), BF16))
            + semaphores(5 + 2 * (rows // BLOCK)),
            moved=200,
        ),
        send_row, boards, returned, dtable, slope, q_weight, djoined, proj_board,
    )
    w_sum.reduce(order)
    late_sum.reduce(order)
    w_sum.reduce(order)
    late_sum.reduce(order)
    w_sum.turn(order)
    late_sum.reduce(order)
    w_sum.gather(order)
    late_sum.turn(order)
    w_sum.gather(order)
    late_sum.gather(order)
    w_sum.gather(order)
    late_sum.gather(order)
    late_sum.gather(order)
    w_sum.last(order)
    w_sizes, late_sizes = [width // 16], [width // 32, lowered // 32]
    grad_w = order(lambda b, m: ordered(b, m, w_sizes, False), bits, w_sum.mine)
    (grad_w,) = order(lambda b, m, o: ordered(b, m, w_sizes, True, o), bits, w_sum.other, grad_w)
    late_sum.last(order)
    both = order(lambda b, m: ordered(b, m, late_sizes, False), bits, late_sum.mine)
    grad_q, grad_proj = order(
        lambda b, m, o: ordered(b, m, late_sizes, True, o), bits, late_sum.other, both
    )
    biases = unpack(jnp.where(core == 0, late_sum.mine[late_rows:], late_sum.other[late_rows:]))
    return (embedding, grad_features, grad_proj, grad_q, biases[0], grad_w, biases[1])


def solution(mesh):
    placed = (
        P(("dom", "rep"), None),
        P(("dom", "rep")),
        P(("dom", "rep"), None),
        P(("dom", "rep"), None),
        P(("dom", "rep")),
        P(("dom", "rep")),
        P(),
        P(),
        P(),
        P(),
        P(),
        P(("dom", "rep"), None),
    )
    return jax.shard_map(
        per_device,
        mesh=mesh,
        in_specs=placed,
        out_specs=(P(("dom", "rep"), None), P(("dom", "rep"), None), P(), P(), P(), P(), P()),
        check_vma=False,
    )
```

```python
import functools

import jax
import jax.numpy as jnp
from jax import lax
from jax.experimental import pallas as pl
from jax.experimental.pallas import tpu as pltpu
from jax.sharding import PartitionSpec as P

F32 = jnp.float32
BF16 = jnp.bfloat16
LANES = 128
BLOCK = 512
MEGA = 1024 * 1024
MARK = 64.0
PLACES = 16
BIAS_ROWS = 16
ROWS_ROWS = (((0,), (0,)), ((), ()))
COLS_COLS = (((1,), (1,)), ((), ()))
VMEM = pl.BlockSpec(memory_space=pltpu.VMEM)
SMEM = pl.BlockSpec(memory_space=pltpu.SMEM)
ANY = pl.BlockSpec(memory_space=pl.ANY)


COST = pl.CostEstimate(flops=0, bytes_accessed=0, transcendentals=0)


def dot(left, right):
    return jnp.dot(left, right, preferred_element_type=F32)


def contract_rows(left, right):
    return lax.dot_general(left, right, ROWS_ROWS, preferred_element_type=F32)


def contract_cols(left, right):
    return lax.dot_general(left, right, COLS_COLS, preferred_element_type=F32)


def whole(*shape):
    return pl.BlockSpec(shape, lambda *_: (0,) * len(shape), pipeline_mode=pl.Buffered(1))


def shape(dims, dtype):
    return jax.ShapeDtypeStruct(dims, dtype)


def call(kernel, outs, in_specs, out_specs, scratch, tokens=(), moved=0, **more):
    count, extra = len(in_specs), len(tokens)

    def run(*refs):
        return kernel(*refs[:count], *refs[count + extra :])

    built = pl.pallas_call(
        run,
        out_shape=outs,
        in_specs=list(in_specs) + [ANY] * extra,
        out_specs=out_specs,
        scratch_shapes=list(scratch),
        compiler_params=pltpu.CompilerParams(vmem_limit_bytes=60 * MEGA),
        cost_estimate=pl.CostEstimate(flops=0, bytes_accessed=moved * MEGA, transcendentals=0),
    )
    return lambda *operands: built(*operands, *tokens)


class Copies:
    def __init__(self, arrived):
        self.arrived = arrived
        self.used = 0

    def start(self, source, target):
        copy = pltpu.make_async_copy(source, target, self.arrived.at[self.used])
        self.used += 1
        copy.start()
        return copy

    def by_blocks(self, source, target, start=True):
        first, count = self.used, source.shape[0] // BLOCK
        self.used += count

        def block(step):
            here = rows_of(step)
            return pltpu.make_async_copy(
                source.at[here], target.at[here], self.arrived.at[first + step]
            )

        if start:
            each_block(count, lambda step: block(step).start())
        return block


def rows_of(step):
    return pl.ds(pl.multiple_of(step * BLOCK, BLOCK), BLOCK)


def each_block(count, body):
    def run(step, _):
        body(step)
        return 0

    lax.fori_loop(0, count, run, 0)


def sigmoid(value):
    return 0.5 * jnp.tanh(0.5 * value) + 0.5


def add_up(low):
    rows, width = low.shape
    return jnp.sum(low.astype(F32).reshape(rows // 8, 8, width), axis=0)


def outgoing_kernel(send, board, features_hbm, out, features, arrived):
    got = pltpu.make_async_copy(features_hbm, features, arrived.at[0])
    got.start()
    rows, width = features.shape
    size = min(512, out.shape[0])
    for step in range(out.shape[0] // size):
        here = slice(step * size, step * size + size)
        names = jnp.broadcast_to(send[:, here], (LANES, size)).T
        lane = lax.broadcasted_iota(jnp.int32, (size, LANES), 1)
        match = [names == lane + first for first in range(0, rows, LANES)]
        hot = jnp.concatenate([jnp.where(m, 1.0, 0.0) for m in match], axis=1)
        kinds = jnp.sum(hot * board[...].astype(F32), axis=1, keepdims=True)
        if step == 0:
            got.wait()
        picked = dot(hot.astype(BF16), features[...])
        last = width - LANES
        out[here, :last] = picked[:, :last].astype(BF16)
        marked = (kinds > 0.5) & (lane == LANES - 1)
        out[here, last:] = jnp.where(marked, MARK, picked[:, last:]).astype(BF16)


def local_kernel(
    names, weights, kinds, q_bias, w_bias, features_hbm, proj_hbm, q_hbm, w_hbm,
    near_hbm, far_hbm, hidden_hbm, slope_hbm, agg_hbm, base_hbm, lowered_hbm, boards,
    features, proj, q_weight, w_top, near, far, hidden, active, slope, agg, base, masked, arrived,
):
    copies = Copies(arrived)
    rows, width = features.shape
    lowered = proj.shape[0]
    got = [
        copies.start(features_hbm, features),
        copies.start(proj_hbm, proj),
        copies.start(q_hbm, q_weight),
    ]
    got_w = copies.start(w_hbm.at[:width], w_top)
    slots = names.shape[1]
    near_heights = near.shape[1] // LANES
    heights = near_heights + far.shape[1] // LANES

    def eight(group):
        name = names[pl.ds(group, 1), :]
        lane = lax.broadcasted_iota(jnp.int32, (LANES, slots), 0)
        hot = jnp.where(lane == (name & (LANES - 1)), 1.0, 0.0).astype(BF16)
        node = lax.broadcasted_iota(jnp.int32, (1, slots), 1) // (slots // 8)
        key = (name >> 7) * 8 + node
        row = lax.broadcasted_iota(jnp.int32, (8 * heights, slots), 0)
        held = jnp.where(row == key, weights[pl.ds(group, 1), :], 0.0)
        return contract_cols(held.astype(BF16), hot)

    def pair(step, _):
        first, second = eight(2 * step), eight(2 * step + 1)
        place = pl.ds(pl.multiple_of(16 * step, 16), 16)
        for h in range(heights):
            both = jnp.concatenate([first[8 * h : 8 * h + 8], second[8 * h : 8 * h + 8]], axis=0)
            if h < near_heights:
                near[place, h * LANES : (h + 1) * LANES] = both.astype(BF16)
            else:
                at = h - near_heights
                far[place, at * LANES : (at + 1) * LANES] = both.astype(BF16)
        return 0

    lax.fori_loop(0, names.shape[0] // 2, pair, 0, unroll=4)
    out = [copies.start(near, near_hbm), copies.start(far, far_hbm)]
    for copy in got:
        copy.wait()
    count = rows // BLOCK

    def front(step):
        here = rows_of(step)
        own = features[here]
        low = own[:, :lowered]
        is_board = kinds[here] == 1
        boards[here] = jnp.where(is_board, jnp.ones((BLOCK, LANES), F32), 0.0)
        masked[here] = jnp.where(is_board, low, jnp.zeros_like(low))
        left = jnp.where(is_board, dot(low, proj[...]), own.astype(F32)).astype(BF16)
        hidden[here] = left
        pre = dot(left, q_weight[...]) + q_bias[...]
        sigma = sigmoid(pre)
        active[here] = (pre * sigma).astype(BF16)
        slope[here] = sigma + pre * sigma * (1.0 - sigma)

    each_block(count, front)
    out += [copies.start(hidden, hidden_hbm), copies.start(slope, slope_hbm)]
    out += [copies.start(masked, lowered_hbm)]
    got_w.wait()
    agg_out = copies.by_blocks(agg, agg_hbm, start=False)
    base_out = copies.by_blocks(base, base_hbm, start=False)

    def local(step):
        here = rows_of(step)
        agg[here] = dot(near[here], active[...]).astype(BF16)
        agg_out(step).start()
        base[here] = dot(hidden[here], w_top[...]) + w_bias[...]
        base_out(step).start()

    each_block(count, local)
    for copy in out:
        copy.wait()
    each_block(count, lambda step: agg_out(step).wait())
    each_block(count, lambda step: base_out(step).wait())


def combine_kernel(
    live, bits, weight, q_bias, far_hbm, incoming_hbm, proj_hbm, q_hbm, agg_hbm, base_hbm, w_hbm,
    cotangent_hbm, hidden_hbm,
    embedding_hbm, dpre2_hbm, dagg_hbm, to_peers_hbm, w_sent_hbm, w_kept_hbm, far_hidden_hbm,
    far_dpre_hbm, far_lowered_hbm, far_slope_hbm, bias,
    far, incoming, proj, q_weight, agg, base, w_low, cotangent, hidden, mean, dpre2, dagg, to_peers,
    w_sent, w_kept, far_hidden, far_slope, far_lowered, arrived,
):
    copies = Copies(arrived)
    rows, width = agg.shape
    count = rows // BLOCK
    got_front = [copies.start(incoming_hbm, incoming), copies.start(proj_hbm, proj)]
    got_front += [copies.start(q_hbm, q_weight)]
    got = [copies.start(far_hbm, far), copies.start(w_hbm.at[width:], w_low)]
    got_agg = copies.by_blocks(agg_hbm, agg)
    got_base = copies.by_blocks(base_hbm, base)
    got_cotangent = copies.by_blocks(cotangent_hbm, cotangent)
    got_hidden = copies.start(hidden_hbm, hidden)
    embedding = base
    embedding_out = copies.by_blocks(embedding, embedding_hbm, start=False)
    dpre2_out = copies.by_blocks(dpre2, dpre2_hbm, start=False)
    dagg_out = copies.by_blocks(dagg, dagg_hbm, start=False)
    outs = [embedding_out, dpre2_out, dagg_out]
    bias[...] = jnp.zeros(bias.shape, F32)
    for copy in got_front:
        copy.wait()
    lowered = proj.shape[0]
    active = incoming
    held = far_hidden.shape[0] == far.shape[1]

    def move(*pairs):
        for i, (source, target) in enumerate(pairs):
            copy = pltpu.make_async_copy(source, target, arrived.at[arrived.shape[0] - 1 - i])
            copy.start()
            copy.wait()

    def front(step):
        here = rows_of(step)
        spot = here if held else pl.ds(0, BLOCK)
        own = incoming[here]
        is_board = own[:, width - 1 :].astype(F32) > MARK / 2
        low = own[:, :lowered]
        far_lowered[spot] = jnp.where(is_board, low, jnp.zeros_like(low))
        left = jnp.where(is_board, dot(low, proj[...]), own.astype(F32)).astype(BF16)
        far_hidden[spot] = left
        pre = dot(left, q_weight[...]) + q_bias[...]
        sigma = sigmoid(pre)
        active[here] = (pre * sigma).astype(BF16)
        far_slope[spot] = sigma + pre * sigma * (1.0 - sigma)
        if not held:
            move(
                (far_lowered, far_lowered_hbm.at[here]),
                (far_hidden, far_hidden_hbm.at[here]),
                (far_slope, far_slope_hbm.at[here]),
            )

    each_block(far.shape[1] // BLOCK, front)
    far_out = []
    if held:
        far_out += [copies.start(far_hidden, far_hidden_hbm)]
        far_out += [copies.start(far_lowered, far_lowered_hbm)]
    for copy in got:
        copy.wait()

    def node_block(step):
        here = rows_of(step)
        got_agg(step).wait()
        total = agg[here].astype(F32) + dot(far[here], active[...])
        average = (total * weight[here]).astype(BF16)
        mean[here] = average
        got_base(step).wait()
        pre = base[here] + dot(average, w_low[...])
        got_cotangent(step).wait()
        sigma = sigmoid(pre)
        post = pre * sigma
        scale = lax.rsqrt(jnp.sum(post * post, axis=1, keepdims=True) + 1e-06)
        row = lax.broadcasted_iota(jnp.int32, (BLOCK, 1), 0) + step * BLOCK
        scale = jnp.where(row < live[0], scale, 0.0)
        embedding[here] = post * scale
        grad = cotangent[here].astype(F32)
        lean = scale * scale * scale * jnp.sum(post * grad, axis=1, keepdims=True)
        dpost = scale * grad - post * lean
        low = (dpost * (sigma + post * (1.0 - sigma))).astype(BF16)
        dpre2[here] = low
        bias[...] += add_up(low)
        dagg[here] = (contract_cols(low, w_low[...]) * weight[here]).astype(BF16)
        for out in outs:
            out(step).start()

    each_block(count, node_block)
    far_dpre = far_hidden
    if held:
        far_out.pop(0).wait()

    def peer_block(step):
        here = rows_of(step)
        spot = here if held else pl.ds(0, BLOCK)
        if not held:
            move((far_slope_hbm.at[here], far_slope))
        table = contract_rows(far[:, here], dagg[...])
        to_peers[spot] = table.astype(BF16)
        far_dpre[spot] = (table * far_slope[spot]).astype(BF16)
        if not held:
            move((to_peers, to_peers_hbm.at[here]), (far_dpre, far_dpre_hbm.at[here]))

    each_block(far.shape[1] // BLOCK, peer_block)
    if held:
        far_out += [copies.start(to_peers, to_peers_hbm), copies.start(far_dpre, far_dpre_hbm)]
    got_hidden.wait()
    stride = width // PLACES
    for target, target_hbm, mark, low in ((w_sent, w_sent_hbm, 2, 1), (w_kept, w_kept_hbm, 1, 0)):

        @pl.when(bits[0] == low)
        def _():
            write_pieces(bits[mark], [(hidden, 0, dpre2)], width, target, stride, 0)

        @pl.when(bits[0] != low)
        def _():
            write_pieces(bits[mark], [(mean, 0, dpre2)], width, target, stride, 0)

        far_out += [copies.start(target, target_hbm)]
    for copy in far_out:
        copy.wait()
    for out in outs:
        each_block(count, lambda step, out=out: out(step).wait())


def write_pieces(mark, pairs, depth, out, stride, at, plus=None):
    piece = depth // PLACES
    size = min(BLOCK, depth)

    def block(step):
        product = 0.0
        for left, first, right in pairs:
            here = pl.ds(pl.multiple_of(first + step * size, size), size)
            product += contract_rows(left[:, here], right[...])
        write_block(mark, product, step * (size // piece), out, stride, at, piece, plus)

    each_block(depth // size, block)


def write_block(mark, product, first, out, stride, at, piece, plus=None):
    for j in range(product.shape[0] // piece):
        place = (first + j) ^ mark
        here = pl.ds(pl.multiple_of(place * stride + at, 16), piece)
        part = product[j * piece : (j + 1) * piece]
        if plus is not None:
            part += plus[here].astype(F32)
        out[here] = part.astype(out.dtype)


def gradients_kernel(
    bits, w_bias, near_hbm, dagg_hbm, slope_hbm, dpre2_hbm, w_hbm, hidden_hbm,
    far_hidden_hbm, far_dpre_hbm, lowered_hbm, far_lowered_hbm, q_hbm,
    dtable_hbm, djoined_hbm, sent_hbm, kept_hbm,
    near, dagg, slope, dpre2, w_top, hidden, far_hidden, far_dpre, lowered, far_lowered,
    q_weight, dtable, djoined, dpre, sent, kept, bias, arrived,
):
    copies = Copies(arrived)
    rows, width = dpre.shape
    depth = lowered.shape[1]
    half = width // 2
    count = rows // BLOCK
    got_table = [copies.start(dagg_hbm, dagg), copies.start(near_hbm, near)]
    got_slope = copies.by_blocks(slope_hbm, slope)
    got_q = [copies.start(hidden_hbm, hidden), copies.start(far_hidden_hbm, far_hidden)]
    got_q += [copies.start(far_dpre_hbm, far_dpre)]
    got_joined = [copies.start(w_hbm.at[:width], w_top), copies.start(dpre2_hbm, dpre2)]
    got_p = [copies.start(lowered_hbm, lowered), copies.start(far_lowered_hbm, far_lowered)]
    got_p += [copies.start(q_hbm, q_weight)]
    bias[...] = jnp.zeros(bias.shape, F32)
    for copy in got_table:
        copy.wait()

    def table_block(step):
        here = rows_of(step)
        table = contract_rows(near[:, here], dagg[...])
        dtable[here] = table.astype(BF16)
        got_slope(step).wait()
        low = (table * slope[here]).astype(BF16)
        dpre[here] = low
        bias[...] += add_up(low)

    each_block(count, table_block)
    out = [copies.start(dtable, dtable_hbm)]
    for copy in got_q:
        copy.wait()

    def far_block(step):
        bias[...] += add_up(far_dpre[rows_of(step)])

    each_block(far_dpre.shape[0] // BLOCK, far_block)
    stride = (half + depth // 2) // PLACES
    sides = ((sent, sent_hbm, 1 - bits[0], bits[2]), (kept, kept_hbm, bits[0], bits[1]))

    def write_q(target, side, mark):
        first = side * half
        pairs = [(hidden, first, dpre), (far_hidden, first, far_dpre)]
        write_pieces(mark, pairs, half, target, stride, 0)

    def write_p(target, side, mark):
        here = pl.ds(pl.multiple_of(side * (depth // 2), depth // 2), depth // 2)
        part = lowered[:, here]
        through = contract_rows(part, dpre[...]) + contract_rows(far_lowered[:, here], far_dpre[...])
        product = contract_cols(through.astype(BF16), q_weight[...])
        product += contract_rows(part, djoined[...])
        write_block(mark, product, 0, target, stride, half // PLACES, depth // 2 // PLACES)

    write_q(sent, *sides[0][2:])
    for copy in got_joined:
        copy.wait()

    def joined_block(step):
        here = rows_of(step)
        djoined[here] = contract_cols(dpre2[here], w_top[...]).astype(BF16)

    each_block(count, joined_block)
    out += [copies.start(djoined, djoined_hbm)]
    for copy in got_p:
        copy.wait()
    write_p(sent, *sides[0][2:])
    row = lax.broadcasted_iota(jnp.int32, (BIAS_ROWS, 1), 0)
    block = jnp.zeros((BIAS_ROWS, width), F32)
    for i, part in enumerate((bias, w_bias)):
        total = jnp.sum(part[...], axis=0, keepdims=True)
        high = total.astype(BF16).astype(F32)
        block = jnp.where(row == i, high, jnp.where(row == i + 2, total - high, block))
    sent[sent.shape[0] - BIAS_ROWS :] = block.astype(BF16)
    out += [copies.start(sent, sent_hbm)]
    write_q(kept, *sides[1][2:])
    write_p(kept, *sides[1][2:])
    out += [copies.start(kept, kept_hbm)]
    for copy in out:
        copy.wait()


def grad_features_kernel(
    send, boards, returned_hbm, dtable_hbm, slope_hbm, q_hbm, djoined_hbm, proj_hbm, grad_hbm,
    returned, dtable, slope, q_weight, djoined, proj, arrived,
):
    copies = Copies(arrived)
    rows = dtable.shape[0]
    lowered = proj.shape[0]
    count = rows // BLOCK
    got = [copies.start(returned_hbm, returned), copies.start(dtable_hbm, dtable)]
    for copy in got:
        copy.wait()
    got_slope = copies.by_blocks(slope_hbm, slope)
    got = [copies.start(q_hbm, q_weight), copies.start(djoined_hbm, djoined)]
    got += [copies.start(proj_hbm, proj)]
    grad_out = copies.by_blocks(slope, grad_hbm, start=False)

    def own_block(step):
        here = rows_of(step)
        row = lax.broadcasted_iota(jnp.int32, (BLOCK, send.shape[1]), 0) + step * BLOCK
        hot = jnp.where(row == send[...], 1.0, 0.0).astype(BF16)
        owned = dtable[here].astype(F32) + dot(hot, returned[...])
        got_slope(step).wait()
        dtable[here] = (owned * slope[here]).astype(BF16)

    each_block(count, own_block)
    for copy in got:
        copy.wait()

    def block(step):
        here = rows_of(step)
        low = contract_cols(dtable[here], q_weight[...]) + djoined[here].astype(F32)
        low = low.astype(BF16)
        product = contract_cols(low, proj[...])
        is_board = boards[here, :1] > 0.5
        own = low.astype(F32)
        slope[here, :lowered] = jnp.where(is_board, product, own[:, :lowered])
        slope[here, lowered:] = jnp.where(is_board, 0.0, own[:, lowered:])
        grad_out(step).start()

    each_block(count, block)
    each_block(count, lambda step: grad_out(step).wait())


def ordered_kernel(bits, held, *refs, count, other):
    outs = refs[-count:]
    mark = bits[2 if other else 1] % 4
    stride = held.shape[0] // 4
    first = 0
    for out in outs:
        piece = out.shape[0] // 4
        for j in range(4):
            here = pl.ds(pl.multiple_of((j ^ mark) * stride + first, 16), piece)
            out[j * piece : (j + 1) * piece] = held[here].astype(F32)
        first += piece


def ordered(bits, held, sizes, other, into=None, part=0, parts=1):
    columns = held.shape[1]
    steps = PLACES // 4
    into = list(into or ())
    mark = 2 if other else 1

    def target(i, b):
        block = (part * (steps // parts) + i) ^ (b[mark] // 4)
        return ((1 - b[0] if other else b[0]) * steps + block, 0)

    return pl.pallas_call(
        functools.partial(ordered_kernel, count=len(sizes), other=other),
        out_shape=[shape((2 * PLACES * size, columns), F32) for size in sizes],
        grid_spec=pltpu.PrefetchScalarGridSpec(
            num_scalar_prefetch=1,
            grid=(steps // parts,),
            in_specs=[pl.BlockSpec((4 * sum(sizes), columns), lambda i, b: (i, 0))]
            + [ANY] * len(into),
            out_specs=[pl.BlockSpec((4 * size, columns), target) for size in sizes],
        ),
        input_output_aliases={2 + i: i for i in range(len(into))},
        compiler_params=pltpu.CompilerParams(vmem_limit_bytes=24 * MEGA),
        cost_estimate=COST,
    )(bits, held, *into)


def swap(value, axis, mask):
    size = lax.axis_size(axis)
    return lax.ppermute(value, axis, [(s, s ^ mask) for s in range(size)])


WAYS = (
    (("dom", 1), ("rep", 2)),
    (("rep", 2), ("dom", 1)),
    (("dom", 2), ("dom", 4)),
    (("dom", 4), ("dom", 2)),
)
FAR_WAYS = WAYS[3], WAYS[2], (("dom", 6), ("dom", 6))


def cross(value, ways):
    doms, reps = lax.axis_size("dom"), lax.axis_size("rep")
    pairs = []
    for d in range(doms):
        for r in range(reps):
            axis, mask = ways[r % 2]
            to = (d ^ mask, r) if axis == "dom" else (d, r ^ mask)
            pairs.append((d * reps + r, to[0] * reps + to[1]))
    return lax.ppermute(value, ("dom", "rep"), pairs)


class Order:
    def __init__(self):
        self.last = ()

    def __call__(self, step, *operands):
        held, _ = lax.optimization_barrier((operands, self.last))
        result = step(*held)
        self.last = jax.tree.leaves(result)[:1]
        return result


def pack(bias):
    high = lax.reduce_precision(bias, 8, 7)
    rest = jnp.zeros((BIAS_ROWS - 4, bias.shape[1]), F32)
    return jnp.concatenate([high, bias - high, rest]).astype(BF16)


def unpack(rows):
    rows = rows[-BIAS_ROWS:].astype(F32)
    return rows[:2] + rows[2:4]


def split_kernel(*refs, with_bias):
    held, back = refs[:2]
    away, stay = refs[-2:]
    half = stay.shape[0]
    size = 64

    def block(step):
        here = pl.ds(pl.multiple_of(step * size, size), size)
        there = pl.ds(pl.multiple_of(half + step * size, size), size)
        stay[here] = held[here].astype(F32) + back[here].astype(F32)
        away[here] = (held[there].astype(F32) + back[there].astype(F32)).astype(BF16)

    each_block(half // size, block)
    if with_bias:
        mine = refs[2][...].astype(F32)
        other = back[2 * half :].astype(F32)
        total = mine[0:2] + mine[2:4] + (other[0:2] + other[2:4])
        total = jnp.concatenate([total, total] + [jnp.zeros((12, total.shape[1]), F32)])
        high = total.astype(BF16).astype(F32)
        row = lax.broadcasted_iota(jnp.int32, total.shape, 0)
        rest = jnp.where(row < 4, total - high, 0.0)
        away[half:] = jnp.where(row < 2, high, rest).astype(BF16)


def split(held, back, *mine):
    half, width = held.shape[0] // 2, held.shape[1]
    return pl.pallas_call(
        functools.partial(split_kernel, with_bias=bool(mine)),
        out_shape=(
            shape((half + len(mine) * BIAS_ROWS, width), BF16), shape((half, width), F32)
        ),
        in_specs=[VMEM] * (2 + len(mine)),
        out_specs=(VMEM, VMEM),
        compiler_params=pltpu.CompilerParams(vmem_limit_bytes=16 * MEGA),
        cost_estimate=COST,
    )(held, back, *mine)


class PieceSum:
    def __init__(self, sent, with_bias):
        self.got = swap(sent, "rep", 1)
        self.bias = None
        self.mine = (sent[-BIAS_ROWS:],) if with_bias else ()
        self.stage = 0

    def first(self, order, kept):
        away, self.held = order(split, kept, self.got, *self.mine)
        self.bias = unpack(away) if self.mine else None
        self.back = cross(away, WAYS[0])

    def reduce(self, order):
        self.stage += 1
        self.split(order, self.held, self.back)

    def split(self, order, held, back):
        half = held.shape[0] // 2

        def step(held, back, bias):
            stay = held[:half].astype(F32) + back[:half].astype(F32)
            away = (held[half:].astype(F32) + back[half : 2 * half].astype(F32)).astype(BF16)
            if bias is not None:
                bias = bias + unpack(back)
                away = jnp.concatenate([away, pack(bias)])
                bias = unpack(away)
            return away, stay, bias

        away, self.held, self.bias = order(step, held, back, self.bias)
        self.back = cross(away, WAYS[self.stage])

    def reduce_far(self, order):
        part = self.held.shape[0] // 4

        def step(held, back, bias):
            stay = held[:part] + back[:part].astype(F32)
            if bias is not None:
                bias = bias + unpack(back)
                packed = pack(bias)
                bias = unpack(packed)
            aways = []
            for i in (1, 2, 3):
                here = slice(i * part, (i + 1) * part)
                away = (held[here] + back[here].astype(F32)).astype(BF16)
                aways.append(away if bias is None else jnp.concatenate([away, packed]))
            return aways, stay, bias

        aways, self.held, self.bias = order(step, self.held, self.back, self.bias)
        self.back = [cross(away, way) for away, way in zip(aways, FAR_WAYS)]

    def turn_far(self, order):
        rows = self.held.shape[0]

        def step(held, back, bias):
            total = held + sum(b[:rows].astype(F32) for b in back)
            if bias is not None:
                got = [unpack(b) for b in back]
                bias = (bias + got[0]) + (got[1] + got[2])
            return total.astype(BF16), bias

        total, self.bias = order(step, self.held, self.back, self.bias)
        self.held = self.beyond(total)
        self.back = [cross(self.held, way) for way in FAR_WAYS]

    def gather_far(self, order):
        self.held = order(lambda h, b: jnp.concatenate([h] + list(b)), self.held, self.back)
        self.back = cross(self.held, WAYS[self.stage])

    def beyond(self, total):
        mask = 8
        while mask < lax.axis_size("dom"):
            total = (total.astype(F32) + swap(total, "dom", mask).astype(F32)).astype(BF16)
            if self.bias is not None:
                self.bias = self.bias + swap(self.bias, "dom", mask)
            mask *= 2
        return total

    def turn(self, order):
        rows = self.held.shape[0]

        def step(held, back, bias):
            total = (held + back[:rows].astype(F32)).astype(BF16)
            return total, None if bias is None else bias + unpack(back)

        total, self.bias = order(step, self.held, self.back, self.bias)
        self.held = self.beyond(total)
        self.back = cross(self.held, WAYS[self.stage])

    def gather(self, order):
        self.held = order(lambda *parts: jnp.concatenate(parts), self.held, self.back)
        self.stage -= 1
        self.back = cross(self.held, WAYS[self.stage])

    def last(self, order):
        self.mine = order(lambda *parts: jnp.concatenate(parts), self.held, self.back)
        self.other = swap(self.mine, "rep", 1)

    def gather_last(self, order):
        extra = [] if self.bias is None else [pack(self.bias)]
        rows = self.held.shape[0] + self.back.shape[0]
        self.mine = order(lambda *parts: jnp.concatenate(parts), self.held, self.back, *extra)
        self.stage -= 1
        self.back = cross(self.mine[:rows], WAYS[self.stage])
        self.other = swap(self.mine, "rep", 1)

    def last_half(self, order):
        self.back = order(lambda value: value, self.back)
        self.other_back = swap(self.back, "rep", 1)


def per_device(
    features,
    node_type,
    neighbours,
    importance,
    send_rows,
    live_rows,
    proj_board,
    q_weight,
    q_bias,
    w_weight,
    w_bias,
    cotangent,
):
    rows, width = features.shape
    lowered = proj_board.shape[0]
    halo = send_rows.shape[0]
    slots = importance.shape[1]
    dom = lax.axis_index("dom")
    rep = lax.axis_index("rep")
    core, y, x, z = rep % 2, rep // 2 % 2, dom % 2, dom // 2 % 4
    low_z, high_z = z % 2, z // 2
    marks = x * 8 + y * 4 + low_z * 2 + high_z, y * 8 + x * 4 + high_z * 2 + low_z
    own, sibling = jnp.where(core == 0, marks[0], marks[1]), jnp.where(core == 0, marks[1], marks[0])
    bits = jnp.stack([core, own, sibling]).astype(jnp.int32)
    send_row = send_rows.reshape(1, halo)
    board_row = node_type.reshape(1, rows)
    kinds = node_type.reshape(rows, 1)
    q_bias_row = q_bias.reshape(1, width)
    w_bias_row = w_bias.reshape(1, width)
    low = (rows, width)
    half = width // 2

    def buffers(*dims):
        return [pltpu.VMEM(d, kind) for d, kind in dims]

    def semaphores(count):
        return [pltpu.SemaphoreType.DMA((count,))]

    outgoing = call(
        outgoing_kernel,
        shape((halo, width), BF16),
        [whole(1, halo), whole(1, rows), ANY],
        whole(halo, width),
        buffers((low, BF16)) + semaphores(1),
    )(send_row, board_row, features)
    incoming = lax.all_to_all(outgoing, "dom", split_axis=0, concat_axis=0, tiled=True)

    wide = -(-slots // 64) * 64
    pad = ((0, 0), (0, wide - slots))
    names = jnp.pad(neighbours, pad, constant_values=-1).reshape(rows // 8, 8 * wide)
    weights = jnp.pad(importance, pad).reshape(rows // 8, 8 * wide)
    narrow = (rows, lowered)
    near, far, hidden, slope, agg, base, own_lowered, boards = call(
        local_kernel,
        (shape((rows, rows), BF16), shape((rows, halo), BF16), shape(low, BF16))
        + (shape(low, F32), shape(low, BF16), shape(low, F32))
        + (shape(narrow, BF16), shape((rows, LANES), F32)),
        [whole(rows // 8, 8 * wide)] * 2 + [whole(rows, 1)] + [whole(1, width)] * 2 + [ANY] * 4,
        (ANY,) * 7 + (whole(rows, LANES),),
        buffers((low, BF16), ((lowered, width), BF16), ((width, width), BF16))
        + buffers(((width, width), BF16), ((rows, rows), BF16), ((rows, halo), BF16))
        + buffers((low, BF16), (low, BF16), (low, F32), (low, BF16), (low, F32), (narrow, BF16))
        + semaphores(9 + 2 * (rows // BLOCK)),
        tokens=(outgoing,),
    )(names, weights, kinds, q_bias_row, w_bias_row, features, proj_board, q_weight, w_weight)

    weight = (1.0 / jnp.sum(importance, axis=1)).reshape(rows, 1)
    w_dims = (width, width)
    far_low, far_narrow = (halo, width), (halo, lowered)
    spot = halo if halo <= rows else BLOCK
    (
        embedding, dpre2, dagg, to_peers, w_sent, w_kept, far_hidden, far_dpre, far_lowered, _,
        w_bias_part,
    ) = call(
        combine_kernel,
        (shape(low, F32), shape(low, BF16), shape(low, BF16))
        + (shape(far_low, BF16), shape(w_dims, BF16), shape(w_dims, BF16))
        + (shape(far_low, BF16), shape(far_low, BF16), shape(far_narrow, BF16))
        + (shape(far_low if spot < halo else (8, LANES), F32), shape((8, width), F32)),
        [SMEM, SMEM, whole(rows, 1), whole(1, width)] + [ANY] * 9,
        (ANY,) * 10 + (whole(8, width),),
        buffers(((rows, halo), BF16), (far_low, BF16), ((lowered, width), BF16))
        + buffers(((width, width), BF16), (low, BF16), (low, F32), ((width, width), BF16))
        + buffers((low, BF16), (low, BF16), (low, BF16), (low, BF16), (low, BF16))
        + buffers(((spot, width), BF16), (w_dims, BF16), (w_dims, BF16), ((spot, width), BF16))
        + buffers(((spot, width), F32), ((spot, lowered), BF16))
        + semaphores(15 + 6 * (rows // BLOCK)),
    )(
        live_rows, bits, weight, q_bias_row, far, incoming, proj_board, q_weight, agg, base, w_weight,
        cotangent, hidden,
    )
    returned = lax.all_to_all(to_peers, "dom", split_axis=0, concat_axis=0, tiled=True)

    order = Order()
    w_sum = PieceSum(w_sent, False)
    late_rows = (width + lowered) // 2
    sent_dims, kept_dims = (late_rows + BIAS_ROWS, width), (late_rows, width)
    w_sum.first(order, w_kept)
    dtable, djoined, late_sent, late_kept = order(
        call(
            gradients_kernel,
            (shape(low, BF16), shape(low, BF16))
            + (shape(sent_dims, BF16), shape(kept_dims, BF16)),
            [SMEM, whole(8, width)] + [ANY] * 11,
            (ANY,) * 4,
            buffers(((rows, rows), BF16), (low, BF16), (low, F32), (low, BF16))
            + buffers(((width, width), BF16), (low, BF16), (far_low, BF16))
            + buffers((far_low, BF16), (narrow, BF16), (far_narrow, BF16), ((width, width), BF16))
            + buffers((low, BF16), (low, BF16), (low, BF16), (sent_dims, BF16))
            + buffers((kept_dims, BF16), ((8, width), F32))
            + semaphores(16 + rows // BLOCK),
            moved=200,
        ),
        bits, w_bias_part, near, dagg, slope, dpre2, w_weight, hidden, far_hidden, far_dpre,
        own_lowered, far_lowered, q_weight,
    )
    w_sum.reduce(order)
    late_sum = PieceSum(order(lambda sent: sent, late_sent), True)
    returned = order(lambda value: value, returned)
    late_sum.first(order, late_kept)
    w_sizes, late_sizes = [width // 16], [width // 32, lowered // 32]
    grad_features = order(
        call(
            grad_features_kernel,
            shape(low, F32),
            [whole(1, halo), whole(rows, LANES)] + [ANY] * 6,
            ANY,
            buffers((far_low, BF16), (low, BF16), (low, F32), ((width, width), BF16))
            + buffers((low, BF16), ((lowered, width), BF16))
            + semaphores(5 + 2 * (rows // BLOCK)),
            moved=200,
        ),
        send_row, boards, returned, dtable, slope, q_weight, djoined, proj_board,
    )
    w_sum.reduce(order)
    late_sum.reduce(order)
    w_sum.reduce(order)
    late_sum.reduce(order)
    late_sum.reduce(order)
    w_sum.turn(order)
    late_sum.turn(order)
    w_sum.gather(order)
    late_sum.gather(order)
    w_sum.gather(order)
    late_sum.gather(order)
    w_sum.gather(order)
    late_sum.gather_last(order)
    w_sum.last(order)
    grad_w = order(lambda b, m: ordered(b, m, w_sizes, False), bits, w_sum.mine)
    (grad_w,) = order(lambda b, m, o: ordered(b, m, w_sizes, True, o), bits, w_sum.other, grad_w)
    both = order(
        lambda b, m: ordered(b, m, late_sizes, False, None, 0, 2), bits, late_sum.mine
    )
    both = order(
        lambda b, m, o: ordered(b, m, late_sizes, True, o, 0, 2), bits, late_sum.other, both
    )
    late_sum.last_half(order)
    both = order(
        lambda b, m, o: ordered(b, m, late_sizes, False, o, 1, 2), bits, late_sum.back, both
    )
    grad_q, grad_proj = order(
        lambda b, m, o: ordered(b, m, late_sizes, True, o, 1, 2), bits, late_sum.other_back, both
    )
    biases = unpack(jnp.where(core == 0, late_sum.mine[-BIAS_ROWS:], late_sum.other[-BIAS_ROWS:]))
    return (embedding, grad_features, grad_proj, grad_q, biases[0], grad_w, biases[1])


def solution(mesh):
    placed = (
        P(("dom", "rep"), None),
        P(("dom", "rep")),
        P(("dom", "rep"), None),
        P(("dom", "rep"), None),
        P(("dom", "rep")),
        P(("dom", "rep")),
        P(),
        P(),
        P(),
        P(),
        P(),
        P(("dom", "rep"), None),
    )
    return jax.shard_map(
        per_device,
        mesh=mesh,
        in_specs=placed,
        out_specs=(P(("dom", "rep"), None), P(("dom", "rep"), None), P(), P(), P(), P(), P()),
        check_vma=False,
    )
```

```python
import functools

import jax
import jax.numpy as jnp
from jax import lax
from jax.experimental import pallas as pl
from jax.experimental.pallas import tpu as pltpu
from jax.sharding import PartitionSpec as P

F32 = jnp.float32
BF16 = jnp.bfloat16
LANES = 128
BLOCK = 512
MEGA = 1024 * 1024
MARK = 64.0
PLACES = 16
BIAS_ROWS = 16
ROWS_ROWS = (((0,), (0,)), ((), ()))
COLS_COLS = (((1,), (1,)), ((), ()))
VMEM = pl.BlockSpec(memory_space=pltpu.VMEM)
SMEM = pl.BlockSpec(memory_space=pltpu.SMEM)
ANY = pl.BlockSpec(memory_space=pl.ANY)


COST = pl.CostEstimate(flops=0, bytes_accessed=0, transcendentals=0)


def dot(left, right):
    return jnp.dot(left, right, preferred_element_type=F32)


def contract_rows(left, right):
    return lax.dot_general(left, right, ROWS_ROWS, preferred_element_type=F32)


def contract_cols(left, right):
    return lax.dot_general(left, right, COLS_COLS, preferred_element_type=F32)


def whole(*shape):
    return pl.BlockSpec(shape, lambda *_: (0,) * len(shape), pipeline_mode=pl.Buffered(1))


def shape(dims, dtype):
    return jax.ShapeDtypeStruct(dims, dtype)


def call(kernel, outs, in_specs, out_specs, scratch, tokens=(), moved=0, **more):
    count, extra = len(in_specs), len(tokens)

    def run(*refs):
        return kernel(*refs[:count], *refs[count + extra :])

    built = pl.pallas_call(
        run,
        out_shape=outs,
        in_specs=list(in_specs) + [ANY] * extra,
        out_specs=out_specs,
        scratch_shapes=list(scratch),
        compiler_params=pltpu.CompilerParams(vmem_limit_bytes=60 * MEGA),
        cost_estimate=pl.CostEstimate(flops=0, bytes_accessed=moved * MEGA, transcendentals=0),
    )
    return lambda *operands: built(*operands, *tokens)


class Copies:
    def __init__(self, arrived):
        self.arrived = arrived
        self.used = 0

    def start(self, source, target):
        copy = pltpu.make_async_copy(source, target, self.arrived.at[self.used])
        self.used += 1
        copy.start()
        return copy

    def by_blocks(self, source, target, start=True):
        first, count = self.used, source.shape[0] // BLOCK
        self.used += count

        def block(step):
            here = rows_of(step)
            return pltpu.make_async_copy(
                source.at[here], target.at[here], self.arrived.at[first + step]
            )

        if start:
            each_block(count, lambda step: block(step).start())
        return block


def rows_of(step):
    return pl.ds(pl.multiple_of(step * BLOCK, BLOCK), BLOCK)


def each_block(count, body):
    def run(step, _):
        body(step)
        return 0

    lax.fori_loop(0, count, run, 0)


def sigmoid(value):
    return 0.5 * jnp.tanh(0.5 * value) + 0.5


def add_up(low):
    rows, width = low.shape
    return jnp.sum(low.astype(F32).reshape(rows // 8, 8, width), axis=0)


def outgoing_kernel(send, board, features_hbm, out, features, arrived):
    got = pltpu.make_async_copy(features_hbm, features, arrived.at[0])
    got.start()
    rows, width = features.shape
    size = min(512, out.shape[0])
    for step in range(out.shape[0] // size):
        here = slice(step * size, step * size + size)
        names = jnp.broadcast_to(send[:, here], (LANES, size)).T
        lane = lax.broadcasted_iota(jnp.int32, (size, LANES), 1)
        match = [names == lane + first for first in range(0, rows, LANES)]
        hot = jnp.concatenate([jnp.where(m, 1.0, 0.0) for m in match], axis=1)
        kinds = jnp.sum(hot * board[...].astype(F32), axis=1, keepdims=True)
        if step == 0:
            got.wait()
        picked = dot(hot.astype(BF16), features[...])
        last = width - LANES
        out[here, :last] = picked[:, :last].astype(BF16)
        marked = (kinds > 0.5) & (lane == LANES - 1)
        out[here, last:] = jnp.where(marked, MARK, picked[:, last:]).astype(BF16)


def local_kernel(
    names, weights, kinds, q_bias, w_bias, features_hbm, proj_hbm, q_hbm, w_hbm,
    near_hbm, far_hbm, hidden_hbm, slope_hbm, agg_hbm, base_hbm, lowered_hbm, boards,
    features, proj, q_weight, w_top, near, far, hidden, active, slope, agg, base, masked, arrived,
):
    copies = Copies(arrived)
    rows, width = features.shape
    lowered = proj.shape[0]
    got = [
        copies.start(features_hbm, features),
        copies.start(proj_hbm, proj),
        copies.start(q_hbm, q_weight),
    ]
    got_w = copies.start(w_hbm.at[:width], w_top)
    slots = names.shape[1]
    near_heights = near.shape[1] // LANES
    heights = near_heights + far.shape[1] // LANES

    def eight(group):
        name = names[pl.ds(group, 1), :]
        lane = lax.broadcasted_iota(jnp.int32, (LANES, slots), 0)
        hot = jnp.where(lane == (name & (LANES - 1)), 1.0, 0.0).astype(BF16)
        node = lax.broadcasted_iota(jnp.int32, (1, slots), 1) // (slots // 8)
        key = (name >> 7) * 8 + node
        row = lax.broadcasted_iota(jnp.int32, (8 * heights, slots), 0)
        held = jnp.where(row == key, weights[pl.ds(group, 1), :], 0.0)
        return contract_cols(held.astype(BF16), hot)

    def pair(step, _):
        first, second = eight(2 * step), eight(2 * step + 1)
        place = pl.ds(pl.multiple_of(16 * step, 16), 16)
        for h in range(heights):
            both = jnp.concatenate([first[8 * h : 8 * h + 8], second[8 * h : 8 * h + 8]], axis=0)
            if h < near_heights:
                near[place, h * LANES : (h + 1) * LANES] = both.astype(BF16)
            else:
                at = h - near_heights
                far[place, at * LANES : (at + 1) * LANES] = both.astype(BF16)
        return 0

    lax.fori_loop(0, names.shape[0] // 2, pair, 0, unroll=4)
    out = [copies.start(near, near_hbm), copies.start(far, far_hbm)]
    for copy in got:
        copy.wait()
    count = rows // BLOCK

    def front(step):
        here = rows_of(step)
        own = features[here]
        low = own[:, :lowered]
        is_board = kinds[here] == 1
        boards[here] = jnp.where(is_board, jnp.ones((BLOCK, LANES), F32), 0.0)
        masked[here] = jnp.where(is_board, low, jnp.zeros_like(low))
        left = jnp.where(is_board, dot(low, proj[...]), own.astype(F32)).astype(BF16)
        hidden[here] = left
        pre = dot(left, q_weight[...]) + q_bias[...]
        sigma = sigmoid(pre)
        active[here] = (pre * sigma).astype(BF16)
        slope[here] = sigma + pre * sigma * (1.0 - sigma)

    each_block(count, front)
    out += [copies.start(hidden, hidden_hbm), copies.start(slope, slope_hbm)]
    out += [copies.start(masked, lowered_hbm)]
    got_w.wait()
    agg_out = copies.by_blocks(agg, agg_hbm, start=False)
    base_out = copies.by_blocks(base, base_hbm, start=False)

    def local(step):
        here = rows_of(step)
        agg[here] = dot(near[here], active[...]).astype(BF16)
        agg_out(step).start()
        base[here] = dot(hidden[here], w_top[...]) + w_bias[...]
        base_out(step).start()

    each_block(count, local)
    for copy in out:
        copy.wait()
    each_block(count, lambda step: agg_out(step).wait())
    each_block(count, lambda step: base_out(step).wait())


def combine_kernel(
    live, bits, weight, q_bias, far_hbm, incoming_hbm, proj_hbm, q_hbm, agg_hbm, base_hbm, w_hbm,
    cotangent_hbm, hidden_hbm,
    embedding_hbm, dpre2_hbm, dagg_hbm, to_peers_hbm, w_sent_hbm, w_kept_hbm, far_hidden_hbm,
    far_dpre_hbm, far_lowered_hbm, far_slope_hbm, bias,
    far, incoming, proj, q_weight, agg, base, w_low, cotangent, hidden, mean, dpre2, dagg, to_peers,
    w_sent, w_kept, far_hidden, far_slope, far_lowered, arrived,
):
    copies = Copies(arrived)
    rows, width = agg.shape
    count = rows // BLOCK
    got_front = [copies.start(incoming_hbm, incoming), copies.start(proj_hbm, proj)]
    got_front += [copies.start(q_hbm, q_weight)]
    got = [copies.start(far_hbm, far), copies.start(w_hbm.at[width:], w_low)]
    got_agg = copies.by_blocks(agg_hbm, agg)
    got_base = copies.by_blocks(base_hbm, base)
    got_cotangent = copies.by_blocks(cotangent_hbm, cotangent)
    got_hidden = copies.start(hidden_hbm, hidden)
    embedding = base
    embedding_out = copies.by_blocks(embedding, embedding_hbm, start=False)
    dpre2_out = copies.by_blocks(dpre2, dpre2_hbm, start=False)
    dagg_out = copies.by_blocks(dagg, dagg_hbm, start=False)
    outs = [embedding_out, dpre2_out, dagg_out]
    bias[...] = jnp.zeros(bias.shape, F32)
    for copy in got_front:
        copy.wait()
    lowered = proj.shape[0]
    active = incoming
    held = far_hidden.shape[0] == far.shape[1]

    def move(*pairs):
        for i, (source, target) in enumerate(pairs):
            copy = pltpu.make_async_copy(source, target, arrived.at[arrived.shape[0] - 1 - i])
            copy.start()
            copy.wait()

    def front(step):
        here = rows_of(step)
        spot = here if held else pl.ds(0, BLOCK)
        own = incoming[here]
        is_board = own[:, width - 1 :].astype(F32) > MARK / 2
        low = own[:, :lowered]
        far_lowered[spot] = jnp.where(is_board, low, jnp.zeros_like(low))
        left = jnp.where(is_board, dot(low, proj[...]), own.astype(F32)).astype(BF16)
        far_hidden[spot] = left
        pre = dot(left, q_weight[...]) + q_bias[...]
        sigma = sigmoid(pre)
        active[here] = (pre * sigma).astype(BF16)
        far_slope[spot] = sigma + pre * sigma * (1.0 - sigma)
        if not held:
            move(
                (far_lowered, far_lowered_hbm.at[here]),
                (far_hidden, far_hidden_hbm.at[here]),
                (far_slope, far_slope_hbm.at[here]),
            )

    each_block(far.shape[1] // BLOCK, front)
    far_out = []
    if held:
        far_out += [copies.start(far_hidden, far_hidden_hbm)]
        far_out += [copies.start(far_lowered, far_lowered_hbm)]
    for copy in got:
        copy.wait()

    def node_block(step):
        here = rows_of(step)
        got_agg(step).wait()
        total = agg[here].astype(F32) + dot(far[here], active[...])
        average = (total * weight[here]).astype(BF16)
        mean[here] = average
        got_base(step).wait()
        pre = base[here] + dot(average, w_low[...])
        got_cotangent(step).wait()
        sigma = sigmoid(pre)
        post = pre * sigma
        scale = lax.rsqrt(jnp.sum(post * post, axis=1, keepdims=True) + 1e-06)
        row = lax.broadcasted_iota(jnp.int32, (BLOCK, 1), 0) + step * BLOCK
        scale = jnp.where(row < live[0], scale, 0.0)
        embedding[here] = post * scale
        grad = cotangent[here].astype(F32)
        lean = scale * scale * scale * jnp.sum(post * grad, axis=1, keepdims=True)
        dpost = scale * grad - post * lean
        low = (dpost * (sigma + post * (1.0 - sigma))).astype(BF16)
        dpre2[here] = low
        bias[...] += add_up(low)
        dagg[here] = (contract_cols(low, w_low[...]) * weight[here]).astype(BF16)
        for out in outs:
            out(step).start()

    each_block(count, node_block)
    far_dpre = far_hidden
    if held:
        far_out.pop(0).wait()

    def peer_block(step):
        here = rows_of(step)
        spot = here if held else pl.ds(0, BLOCK)
        if not held:
            move((far_slope_hbm.at[here], far_slope))
        table = contract_rows(far[:, here], dagg[...])
        to_peers[spot] = table.astype(BF16)
        far_dpre[spot] = (table * far_slope[spot]).astype(BF16)
        if not held:
            move((to_peers, to_peers_hbm.at[here]), (far_dpre, far_dpre_hbm.at[here]))

    each_block(far.shape[1] // BLOCK, peer_block)
    if held:
        far_out += [copies.start(to_peers, to_peers_hbm), copies.start(far_dpre, far_dpre_hbm)]
    got_hidden.wait()
    stride = width // PLACES
    for target, target_hbm, mark, low in ((w_sent, w_sent_hbm, 2, 1), (w_kept, w_kept_hbm, 1, 0)):

        @pl.when(bits[0] == low)
        def _():
            write_pieces(bits[mark], [(hidden, 0, dpre2)], width, target, stride, 0)

        @pl.when(bits[0] != low)
        def _():
            write_pieces(bits[mark], [(mean, 0, dpre2)], width, target, stride, 0)

        far_out += [copies.start(target, target_hbm)]
    for copy in far_out:
        copy.wait()
    for out in outs:
        each_block(count, lambda step, out=out: out(step).wait())


def write_pieces(mark, pairs, depth, out, stride, at, plus=None):
    piece = depth // PLACES
    size = min(BLOCK, depth)

    def block(step):
        product = 0.0
        for left, first, right in pairs:
            here = pl.ds(pl.multiple_of(first + step * size, size), size)
            product += contract_rows(left[:, here], right[...])
        write_block(mark, product, step * (size // piece), out, stride, at, piece, plus)

    each_block(depth // size, block)


def write_block(mark, product, first, out, stride, at, piece, plus=None):
    for j in range(product.shape[0] // piece):
        place = (first + j) ^ mark
        here = pl.ds(pl.multiple_of(place * stride + at, 16), piece)
        part = product[j * piece : (j + 1) * piece]
        if plus is not None:
            part += plus[here].astype(F32)
        out[here] = part.astype(out.dtype)


def gradients_kernel(
    bits, w_bias, near_hbm, dagg_hbm, slope_hbm, dpre2_hbm, w_hbm, hidden_hbm,
    far_hidden_hbm, far_dpre_hbm, lowered_hbm, far_lowered_hbm, q_hbm,
    dtable_hbm, djoined_hbm, sent_hbm, kept_hbm,
    near, dagg, slope, dpre2, w_top, hidden, far_hidden, far_dpre, lowered, far_lowered,
    q_weight, dtable, djoined, dpre, sent, kept, bias, arrived,
):
    copies = Copies(arrived)
    rows, width = dpre.shape
    depth = lowered.shape[1]
    half = width // 2
    count = rows // BLOCK
    got_table = [copies.start(dagg_hbm, dagg), copies.start(near_hbm, near)]
    got_slope = copies.by_blocks(slope_hbm, slope)
    got_q = [copies.start(hidden_hbm, hidden), copies.start(far_hidden_hbm, far_hidden)]
    got_q += [copies.start(far_dpre_hbm, far_dpre)]
    got_joined = [copies.start(w_hbm.at[:width], w_top), copies.start(dpre2_hbm, dpre2)]
    got_p = [copies.start(lowered_hbm, lowered), copies.start(far_lowered_hbm, far_lowered)]
    got_p += [copies.start(q_hbm, q_weight)]
    bias[...] = jnp.zeros(bias.shape, F32)
    for copy in got_table:
        copy.wait()

    def table_block(step):
        here = rows_of(step)
        table = contract_rows(near[:, here], dagg[...])
        dtable[here] = table.astype(BF16)
        got_slope(step).wait()
        low = (table * slope[here]).astype(BF16)
        dpre[here] = low
        bias[...] += add_up(low)

    each_block(count, table_block)
    out = [copies.start(dtable, dtable_hbm)]
    for copy in got_q:
        copy.wait()

    def far_block(step):
        bias[...] += add_up(far_dpre[rows_of(step)])

    each_block(far_dpre.shape[0] // BLOCK, far_block)
    stride = (half + depth // 2) // PLACES
    sides = ((sent, sent_hbm, 1 - bits[0], bits[2]), (kept, kept_hbm, bits[0], bits[1]))

    def write_q(target, side, mark):
        first = side * half
        pairs = [(hidden, first, dpre), (far_hidden, first, far_dpre)]
        write_pieces(mark, pairs, half, target, stride, 0)

    def write_p(target, side, mark):
        here = pl.ds(pl.multiple_of(side * (depth // 2), depth // 2), depth // 2)
        part = lowered[:, here]
        through = contract_rows(part, dpre[...]) + contract_rows(far_lowered[:, here], far_dpre[...])
        product = contract_cols(through.astype(BF16), q_weight[...])
        product += contract_rows(part, djoined[...])
        write_block(mark, product, 0, target, stride, half // PLACES, depth // 2 // PLACES)

    write_q(sent, *sides[0][2:])
    for copy in got_joined:
        copy.wait()

    def joined_block(step):
        here = rows_of(step)
        djoined[here] = contract_cols(dpre2[here], w_top[...]).astype(BF16)

    each_block(count, joined_block)
    out += [copies.start(djoined, djoined_hbm)]
    for copy in got_p:
        copy.wait()
    write_p(sent, *sides[0][2:])
    row = lax.broadcasted_iota(jnp.int32, (BIAS_ROWS, 1), 0)
    block = jnp.zeros((BIAS_ROWS, width), F32)
    for i, part in enumerate((bias, w_bias)):
        total = jnp.sum(part[...], axis=0, keepdims=True)
        high = total.astype(BF16).astype(F32)
        block = jnp.where(row == i, high, jnp.where(row == i + 2, total - high, block))
    sent[sent.shape[0] - BIAS_ROWS :] = block.astype(BF16)
    out += [copies.start(sent, sent_hbm)]
    write_q(kept, *sides[1][2:])
    write_p(kept, *sides[1][2:])
    out += [copies.start(kept, kept_hbm)]
    for copy in out:
        copy.wait()


def grad_features_kernel(
    send, boards, returned_hbm, dtable_hbm, slope_hbm, q_hbm, djoined_hbm, proj_hbm, grad_hbm,
    returned, dtable, slope, q_weight, djoined, proj, arrived,
):
    copies = Copies(arrived)
    rows = dtable.shape[0]
    lowered = proj.shape[0]
    count = rows // BLOCK
    got = [copies.start(returned_hbm, returned), copies.start(dtable_hbm, dtable)]
    for copy in got:
        copy.wait()
    got_slope = copies.by_blocks(slope_hbm, slope)
    got = [copies.start(q_hbm, q_weight), copies.start(djoined_hbm, djoined)]
    got += [copies.start(proj_hbm, proj)]
    grad_out = copies.by_blocks(slope, grad_hbm, start=False)

    def own_block(step):
        here = rows_of(step)
        row = lax.broadcasted_iota(jnp.int32, (BLOCK, send.shape[1]), 0) + step * BLOCK
        hot = jnp.where(row == send[...], 1.0, 0.0).astype(BF16)
        owned = dtable[here].astype(F32) + dot(hot, returned[...])
        got_slope(step).wait()
        dtable[here] = (owned * slope[here]).astype(BF16)

    each_block(count, own_block)
    for copy in got:
        copy.wait()

    def block(step):
        here = rows_of(step)
        low = contract_cols(dtable[here], q_weight[...]) + djoined[here].astype(F32)
        low = low.astype(BF16)
        product = contract_cols(low, proj[...])
        is_board = boards[here, :1] > 0.5
        own = low.astype(F32)
        slope[here, :lowered] = jnp.where(is_board, product, own[:, :lowered])
        slope[here, lowered:] = jnp.where(is_board, 0.0, own[:, lowered:])
        grad_out(step).start()

    each_block(count, block)
    each_block(count, lambda step: grad_out(step).wait())


def ordered_kernel(bits, held, *refs, count, other):
    outs = refs[-count:]
    mark = bits[2 if other else 1] % 4
    stride = held.shape[0] // 4
    first = 0
    for out in outs:
        piece = out.shape[0] // 4
        for j in range(4):
            here = pl.ds(pl.multiple_of((j ^ mark) * stride + first, 16), piece)
            out[j * piece : (j + 1) * piece] = held[here].astype(F32)
        first += piece


def ordered(bits, held, sizes, other, into=None, part=0, parts=1):
    columns = held.shape[1]
    steps = PLACES // 4
    into = list(into or ())
    mark = 2 if other else 1

    def target(i, b):
        block = (part * (steps // parts) + i) ^ (b[mark] // 4)
        return ((1 - b[0] if other else b[0]) * steps + block, 0)

    return pl.pallas_call(
        functools.partial(ordered_kernel, count=len(sizes), other=other),
        out_shape=[shape((2 * PLACES * size, columns), F32) for size in sizes],
        grid_spec=pltpu.PrefetchScalarGridSpec(
            num_scalar_prefetch=1,
            grid=(steps // parts,),
            in_specs=[pl.BlockSpec((4 * sum(sizes), columns), lambda i, b: (i, 0))]
            + [ANY] * len(into),
            out_specs=[pl.BlockSpec((4 * size, columns), target) for size in sizes],
        ),
        input_output_aliases={2 + i: i for i in range(len(into))},
        compiler_params=pltpu.CompilerParams(vmem_limit_bytes=24 * MEGA),
        cost_estimate=COST,
    )(bits, held, *into)


def swap(value, axis, mask):
    size = lax.axis_size(axis)
    return lax.ppermute(value, axis, [(s, s ^ mask) for s in range(size)])


WAYS = (
    (("dom", 1), ("rep", 2)),
    (("rep", 2), ("dom", 1)),
    (("dom", 2), ("dom", 4)),
    (("dom", 4), ("dom", 2)),
)
FAR_WAYS = WAYS[3], WAYS[2], (("dom", 6), ("dom", 6))


def cross(value, ways):
    doms, reps = lax.axis_size("dom"), lax.axis_size("rep")
    pairs = []
    for d in range(doms):
        for r in range(reps):
            axis, mask = ways[r % 2]
            to = (d ^ mask, r) if axis == "dom" else (d, r ^ mask)
            pairs.append((d * reps + r, to[0] * reps + to[1]))
    return lax.ppermute(value, ("dom", "rep"), pairs)


class Order:
    def __init__(self):
        self.last = ()

    def __call__(self, step, *operands):
        held, _ = lax.optimization_barrier((operands, self.last))
        result = step(*held)
        self.last = jax.tree.leaves(result)[:1]
        return result

    def tick(self):
        def nothing(_, out):
            out[...] = jnp.zeros(out.shape, F32)

        self.last = [
            pl.pallas_call(
                nothing,
                out_shape=shape((8, LANES), F32),
                in_specs=[ANY],
                out_specs=VMEM,
                compiler_params=pltpu.CompilerParams(vmem_limit_bytes=MEGA),
                cost_estimate=COST,
            )(*self.last)
        ]


def pack(bias):
    high = lax.reduce_precision(bias, 8, 7)
    rest = jnp.zeros((BIAS_ROWS - 4, bias.shape[1]), F32)
    return jnp.concatenate([high, bias - high, rest]).astype(BF16)


def unpack(rows):
    rows = rows[-BIAS_ROWS:].astype(F32)
    return rows[:2] + rows[2:4]


def split_kernel(*refs, with_bias):
    held, back = refs[:2]
    away, stay = refs[-2:]
    half = stay.shape[0]
    size = 64

    def block(step):
        here = pl.ds(pl.multiple_of(step * size, size), size)
        there = pl.ds(pl.multiple_of(half + step * size, size), size)
        stay[here] = held[here].astype(F32) + back[here].astype(F32)
        away[here] = (held[there].astype(F32) + back[there].astype(F32)).astype(BF16)

    each_block(half // size, block)
    if with_bias:
        mine = refs[2][...].astype(F32)
        other = back[2 * half :].astype(F32)
        total = mine[0:2] + mine[2:4] + (other[0:2] + other[2:4])
        total = jnp.concatenate([total, total] + [jnp.zeros((12, total.shape[1]), F32)])
        high = total.astype(BF16).astype(F32)
        row = lax.broadcasted_iota(jnp.int32, total.shape, 0)
        rest = jnp.where(row < 4, total - high, 0.0)
        away[half:] = jnp.where(row < 2, high, rest).astype(BF16)


def split(held, back, *mine):
    half, width = held.shape[0] // 2, held.shape[1]
    return pl.pallas_call(
        functools.partial(split_kernel, with_bias=bool(mine)),
        out_shape=(
            shape((half + len(mine) * BIAS_ROWS, width), BF16), shape((half, width), F32)
        ),
        in_specs=[VMEM] * (2 + len(mine)),
        out_specs=(VMEM, VMEM),
        compiler_params=pltpu.CompilerParams(vmem_limit_bytes=16 * MEGA),
        cost_estimate=COST,
    )(held, back, *mine)


class PieceSum:
    def __init__(self, sent, with_bias):
        self.got = swap(sent, "rep", 1)
        self.bias = None
        self.mine = (sent[-BIAS_ROWS:],) if with_bias else ()
        self.stage = 0

    def first(self, order, kept):
        away, self.held = order(split, kept, self.got, *self.mine)
        self.bias = unpack(away) if self.mine else None
        self.back = cross(away, WAYS[0])

    def reduce(self, order):
        self.stage += 1
        self.split(order, self.held, self.back)

    def split(self, order, held, back):
        half = held.shape[0] // 2

        def step(held, back, bias):
            stay = held[:half].astype(F32) + back[:half].astype(F32)
            away = (held[half:].astype(F32) + back[half : 2 * half].astype(F32)).astype(BF16)
            if bias is not None:
                bias = bias + unpack(back)
                away = jnp.concatenate([away, pack(bias)])
                bias = unpack(away)
            return away, stay, bias

        away, self.held, self.bias = order(step, held, back, self.bias)
        self.back = cross(away, WAYS[self.stage])

    def reduce_far(self, order):
        part = self.held.shape[0] // 4

        def step(held, back, bias):
            stay = held[:part] + back[:part].astype(F32)
            if bias is not None:
                bias = bias + unpack(back)
                packed = pack(bias)
                bias = unpack(packed)
            aways = []
            for i in (1, 2, 3):
                here = slice(i * part, (i + 1) * part)
                away = (held[here] + back[here].astype(F32)).astype(BF16)
                aways.append(away if bias is None else jnp.concatenate([away, packed]))
            return aways, stay, bias

        aways, self.held, self.bias = order(step, self.held, self.back, self.bias)
        self.back = [cross(away, way) for away, way in zip(aways, FAR_WAYS)]

    def turn_far(self, order):
        rows = self.held.shape[0]

        def step(held, back, bias):
            total = held + sum(b[:rows].astype(F32) for b in back)
            if bias is not None:
                got = [unpack(b) for b in back]
                bias = (bias + got[0]) + (got[1] + got[2])
            return total.astype(BF16), bias

        total, self.bias = order(step, self.held, self.back, self.bias)
        self.held = self.beyond(total)
        self.back = [cross(self.held, way) for way in FAR_WAYS]

    def gather_far(self, order):
        self.held = order(lambda h, b: jnp.concatenate([h] + list(b)), self.held, self.back)
        self.back = cross(self.held, WAYS[self.stage])

    def beyond(self, total):
        mask = 8
        while mask < lax.axis_size("dom"):
            total = (total.astype(F32) + swap(total, "dom", mask).astype(F32)).astype(BF16)
            if self.bias is not None:
                self.bias = self.bias + swap(self.bias, "dom", mask)
            mask *= 2
        return total

    def turn(self, order):
        rows = self.held.shape[0]

        def step(held, back, bias):
            total = (held + back[:rows].astype(F32)).astype(BF16)
            return total, None if bias is None else bias + unpack(back)

        total, self.bias = order(step, self.held, self.back, self.bias)
        self.held = self.beyond(total)
        self.back = cross(self.held, WAYS[self.stage])

    def gather(self, order):
        self.held = order(lambda *parts: jnp.concatenate(parts), self.held, self.back)
        self.stage -= 1
        self.back = cross(self.held, WAYS[self.stage])

    def last(self, order):
        self.mine = order(lambda *parts: jnp.concatenate(parts), self.held, self.back)
        self.other = swap(self.mine, "rep", 1)

    def gather_last(self, order):
        extra = [] if self.bias is None else [pack(self.bias)]
        rows = self.held.shape[0] + self.back.shape[0]
        self.mine = order(lambda *parts: jnp.concatenate(parts), self.held, self.back, *extra)
        self.stage -= 1
        self.back = cross(self.mine[:rows], WAYS[self.stage])
        self.other = swap(self.mine, "rep", 1)

    def last_half(self, order):
        self.back = order(lambda value: value, self.back)
        self.other_back = swap(self.back, "rep", 1)


def per_device(
    features,
    node_type,
    neighbours,
    importance,
    send_rows,
    live_rows,
    proj_board,
    q_weight,
    q_bias,
    w_weight,
    w_bias,
    cotangent,
):
    rows, width = features.shape
    lowered = proj_board.shape[0]
    halo = send_rows.shape[0]
    slots = importance.shape[1]
    dom = lax.axis_index("dom")
    rep = lax.axis_index("rep")
    core, y, x, z = rep % 2, rep // 2 % 2, dom % 2, dom // 2 % 4
    low_z, high_z = z % 2, z // 2
    marks = x * 8 + y * 4 + low_z * 2 + high_z, y * 8 + x * 4 + high_z * 2 + low_z
    own, sibling = jnp.where(core == 0, marks[0], marks[1]), jnp.where(core == 0, marks[1], marks[0])
    bits = jnp.stack([core, own, sibling]).astype(jnp.int32)
    send_row = send_rows.reshape(1, halo)
    board_row = node_type.reshape(1, rows)
    kinds = node_type.reshape(rows, 1)
    q_bias_row = q_bias.reshape(1, width)
    w_bias_row = w_bias.reshape(1, width)
    low = (rows, width)
    half = width // 2

    def buffers(*dims):
        return [pltpu.VMEM(d, kind) for d, kind in dims]

    def semaphores(count):
        return [pltpu.SemaphoreType.DMA((count,))]

    outgoing = call(
        outgoing_kernel,
        shape((halo, width), BF16),
        [whole(1, halo), whole(1, rows), ANY],
        whole(halo, width),
        buffers((low, BF16)) + semaphores(1),
    )(send_row, board_row, features)
    incoming = lax.all_to_all(outgoing, "dom", split_axis=0, concat_axis=0, tiled=True)

    wide = -(-slots // 64) * 64
    pad = ((0, 0), (0, wide - slots))
    names = jnp.pad(neighbours, pad, constant_values=-1).reshape(rows // 8, 8 * wide)
    weights = jnp.pad(importance, pad).reshape(rows // 8, 8 * wide)
    narrow = (rows, lowered)
    near, far, hidden, slope, agg, base, own_lowered, boards = call(
        local_kernel,
        (shape((rows, rows), BF16), shape((rows, halo), BF16), shape(low, BF16))
        + (shape(low, F32), shape(low, BF16), shape(low, F32))
        + (shape(narrow, BF16), shape((rows, LANES), F32)),
        [whole(rows // 8, 8 * wide)] * 2 + [whole(rows, 1)] + [whole(1, width)] * 2 + [ANY] * 4,
        (ANY,) * 7 + (whole(rows, LANES),),
        buffers((low, BF16), ((lowered, width), BF16), ((width, width), BF16))
        + buffers(((width, width), BF16), ((rows, rows), BF16), ((rows, halo), BF16))
        + buffers((low, BF16), (low, BF16), (low, F32), (low, BF16), (low, F32), (narrow, BF16))
        + semaphores(9 + 2 * (rows // BLOCK)),
        tokens=(outgoing,),
    )(names, weights, kinds, q_bias_row, w_bias_row, features, proj_board, q_weight, w_weight)

    weight = (1.0 / jnp.sum(importance, axis=1)).reshape(rows, 1)
    w_dims = (width, width)
    far_low, far_narrow = (halo, width), (halo, lowered)
    spot = halo if halo <= rows else BLOCK
    (
        embedding, dpre2, dagg, to_peers, w_sent, w_kept, far_hidden, far_dpre, far_lowered, _,
        w_bias_part,
    ) = call(
        combine_kernel,
        (shape(low, F32), shape(low, BF16), shape(low, BF16))
        + (shape(far_low, BF16), shape(w_dims, BF16), shape(w_dims, BF16))
        + (shape(far_low, BF16), shape(far_low, BF16), shape(far_narrow, BF16))
        + (shape(far_low if spot < halo else (8, LANES), F32), shape((8, width), F32)),
        [SMEM, SMEM, whole(rows, 1), whole(1, width)] + [ANY] * 9,
        (ANY,) * 10 + (whole(8, width),),
        buffers(((rows, halo), BF16), (far_low, BF16), ((lowered, width), BF16))
        + buffers(((width, width), BF16), (low, BF16), (low, F32), ((width, width), BF16))
        + buffers((low, BF16), (low, BF16), (low, BF16), (low, BF16), (low, BF16))
        + buffers(((spot, width), BF16), (w_dims, BF16), (w_dims, BF16), ((spot, width), BF16))
        + buffers(((spot, width), F32), ((spot, lowered), BF16))
        + semaphores(15 + 6 * (rows // BLOCK)),
    )(
        live_rows, bits, weight, q_bias_row, far, incoming, proj_board, q_weight, agg, base, w_weight,
        cotangent, hidden,
    )
    returned = lax.all_to_all(to_peers, "dom", split_axis=0, concat_axis=0, tiled=True)

    order = Order()
    w_sum = PieceSum(w_sent, False)
    late_rows = (width + lowered) // 2
    sent_dims, kept_dims = (late_rows + BIAS_ROWS, width), (late_rows, width)
    w_sum.first(order, w_kept)
    dtable, djoined, late_sent, late_kept = order(
        call(
            gradients_kernel,
            (shape(low, BF16), shape(low, BF16))
            + (shape(sent_dims, BF16), shape(kept_dims, BF16)),
            [SMEM, whole(8, width)] + [ANY] * 11,
            (ANY,) * 4,
            buffers(((rows, rows), BF16), (low, BF16), (low, F32), (low, BF16))
            + buffers(((width, width), BF16), (low, BF16), (far_low, BF16))
            + buffers((far_low, BF16), (narrow, BF16), (far_narrow, BF16), ((width, width), BF16))
            + buffers((low, BF16), (low, BF16), (low, BF16), (sent_dims, BF16))
            + buffers((kept_dims, BF16), ((8, width), F32))
            + semaphores(16 + rows // BLOCK),
            moved=200,
        ),
        bits, w_bias_part, near, dagg, slope, dpre2, w_weight, hidden, far_hidden, far_dpre,
        own_lowered, far_lowered, q_weight,
    )
    w_sum.reduce(order)
    late_sum = PieceSum(order(lambda sent: sent, late_sent), True)
    returned = order(lambda value: value, returned)
    late_sum.first(order, late_kept)
    w_sizes, late_sizes = [width // 16], [width // 32, lowered // 32]
    w_sum.reduce(order)
    late_sum.reduce(order)
    w_sum.reduce(order)
    late_sum.reduce(order)
    w_sum.turn(order)
    w_sum.gather(order)
    late_sum.reduce(order)
    late_sum.turn(order)
    w_sum.gather(order)
    late_sum.gather(order)
    late_sum.gather(order)
    w_sum.gather(order)
    grad_features = order(
        call(
            grad_features_kernel,
            shape(low, F32),
            [whole(1, halo), whole(rows, LANES)] + [ANY] * 6,
            ANY,
            buffers((far_low, BF16), (low, BF16), (low, F32), ((width, width), BF16))
            + buffers((low, BF16), ((lowered, width), BF16))
            + semaphores(5 + 2 * (rows // BLOCK)),
            moved=200,
        ),
        send_row, boards, returned, dtable, slope, q_weight, djoined, proj_board,
    )
    late_sum.gather_last(order)
    both = order(
        lambda b, m: ordered(b, m, late_sizes, False, None, 0, 2), bits, late_sum.mine
    )
    w_sum.last(order)
    both = order(
        lambda b, m, o: ordered(b, m, late_sizes, True, o, 0, 2), bits, late_sum.other, both
    )
    grad_w = order(lambda b, m: ordered(b, m, w_sizes, False), bits, w_sum.mine)
    (grad_w,) = order(lambda b, m, o: ordered(b, m, w_sizes, True, o), bits, w_sum.other, grad_w)
    late_sum.last_half(order)
    both = order(
        lambda b, m, o: ordered(b, m, late_sizes, False, o, 1, 2), bits, late_sum.back, both
    )
    grad_q, grad_proj = order(
        lambda b, m, o: ordered(b, m, late_sizes, True, o, 1, 2), bits, late_sum.other_back, both
    )
    biases = unpack(jnp.where(core == 0, late_sum.mine[-BIAS_ROWS:], late_sum.other[-BIAS_ROWS:]))
    return (embedding, grad_features, grad_proj, grad_q, biases[0], grad_w, biases[1])


def solution(mesh):
    placed = (
        P(("dom", "rep"), None),
        P(("dom", "rep")),
        P(("dom", "rep"), None),
        P(("dom", "rep"), None),
        P(("dom", "rep")),
        P(("dom", "rep")),
        P(),
        P(),
        P(),
        P(),
        P(),
        P(("dom", "rep"), None),
    )
    return jax.shard_map(
        per_device,
        mesh=mesh,
        in_specs=placed,
        out_specs=(P(("dom", "rep"), None), P(("dom", "rep"), None), P(), P(), P(), P(), P()),
        check_vma=False,
    )
```

```python
import functools

import jax
import jax.numpy as jnp
from jax import lax
from jax.experimental import pallas as pl
from jax.experimental.pallas import tpu as pltpu
from jax.sharding import PartitionSpec as P

F32 = jnp.float32
BF16 = jnp.bfloat16
LANES = 128
BLOCK = 512
MEGA = 1024 * 1024
MARK = 64.0
PLACES = 16
BIAS_ROWS = 16
ROWS_ROWS = (((0,), (0,)), ((), ()))
COLS_COLS = (((1,), (1,)), ((), ()))
VMEM = pl.BlockSpec(memory_space=pltpu.VMEM)
SMEM = pl.BlockSpec(memory_space=pltpu.SMEM)
ANY = pl.BlockSpec(memory_space=pl.ANY)


COST = pl.CostEstimate(flops=0, bytes_accessed=0, transcendentals=0)


def dot(left, right):
    return jnp.dot(left, right, preferred_element_type=F32)


def contract_rows(left, right):
    return lax.dot_general(left, right, ROWS_ROWS, preferred_element_type=F32)


def contract_cols(left, right):
    return lax.dot_general(left, right, COLS_COLS, preferred_element_type=F32)


def whole(*shape):
    return pl.BlockSpec(shape, lambda *_: (0,) * len(shape), pipeline_mode=pl.Buffered(1))


def shape(dims, dtype):
    return jax.ShapeDtypeStruct(dims, dtype)


def call(kernel, outs, in_specs, out_specs, scratch, tokens=(), moved=0, **more):
    count, extra = len(in_specs), len(tokens)

    def run(*refs):
        return kernel(*refs[:count], *refs[count + extra :])

    built = pl.pallas_call(
        run,
        out_shape=outs,
        in_specs=list(in_specs) + [ANY] * extra,
        out_specs=out_specs,
        scratch_shapes=list(scratch),
        compiler_params=pltpu.CompilerParams(vmem_limit_bytes=60 * MEGA),
        cost_estimate=pl.CostEstimate(flops=0, bytes_accessed=moved * MEGA, transcendentals=0),
    )
    return lambda *operands: built(*operands, *tokens)


class Copies:
    def __init__(self, arrived):
        self.arrived = arrived
        self.used = 0

    def start(self, source, target):
        copy = pltpu.make_async_copy(source, target, self.arrived.at[self.used])
        self.used += 1
        copy.start()
        return copy

    def by_blocks(self, source, target, start=True):
        first, count = self.used, source.shape[0] // BLOCK
        self.used += count

        def block(step):
            here = rows_of(step)
            return pltpu.make_async_copy(
                source.at[here], target.at[here], self.arrived.at[first + step]
            )

        if start:
            each_block(count, lambda step: block(step).start())
        return block


def rows_of(step):
    return pl.ds(pl.multiple_of(step * BLOCK, BLOCK), BLOCK)


def each_block(count, body):
    def run(step, _):
        body(step)
        return 0

    lax.fori_loop(0, count, run, 0)


def sigmoid(value):
    return 0.5 * jnp.tanh(0.5 * value) + 0.5


def add_up(low):
    rows, width = low.shape
    return jnp.sum(low.astype(F32).reshape(rows // 8, 8, width), axis=0)


def outgoing_kernel(send, board, features_hbm, out, features, arrived):
    got = pltpu.make_async_copy(features_hbm, features, arrived.at[0])
    got.start()
    rows, width = features.shape
    size = min(512, out.shape[0])
    for step in range(out.shape[0] // size):
        here = slice(step * size, step * size + size)
        names = jnp.broadcast_to(send[:, here], (LANES, size)).T
        lane = lax.broadcasted_iota(jnp.int32, (size, LANES), 1)
        match = [names == lane + first for first in range(0, rows, LANES)]
        hot = jnp.concatenate([jnp.where(m, 1.0, 0.0) for m in match], axis=1)
        kinds = jnp.sum(hot * board[...].astype(F32), axis=1, keepdims=True)
        if step == 0:
            got.wait()
        picked = dot(hot.astype(BF16), features[...])
        last = width - LANES
        out[here, :last] = picked[:, :last].astype(BF16)
        marked = (kinds > 0.5) & (lane == LANES - 1)
        out[here, last:] = jnp.where(marked, MARK, picked[:, last:]).astype(BF16)


def local_kernel(
    names, weights, kinds, q_bias, w_bias, features_hbm, proj_hbm, q_hbm, w_hbm,
    near_hbm, far_hbm, hidden_hbm, slope_hbm, agg_hbm, base_hbm, lowered_hbm, boards,
    features, proj, q_weight, w_top, near, far, hidden, active, slope, agg, base, masked, arrived,
):
    copies = Copies(arrived)
    rows, width = features.shape
    lowered = proj.shape[0]
    got = [
        copies.start(features_hbm, features),
        copies.start(proj_hbm, proj),
        copies.start(q_hbm, q_weight),
    ]
    got_w = copies.start(w_hbm.at[:width], w_top)
    slots = names.shape[1]
    near_heights = near.shape[1] // LANES
    heights = near_heights + far.shape[1] // LANES

    def eight(group):
        name = names[pl.ds(group, 1), :]
        lane = lax.broadcasted_iota(jnp.int32, (LANES, slots), 0)
        hot = jnp.where(lane == (name & (LANES - 1)), 1.0, 0.0).astype(BF16)
        node = lax.broadcasted_iota(jnp.int32, (1, slots), 1) // (slots // 8)
        key = (name >> 7) * 8 + node
        row = lax.broadcasted_iota(jnp.int32, (8 * heights, slots), 0)
        held = jnp.where(row == key, weights[pl.ds(group, 1), :], 0.0)
        return contract_cols(held.astype(BF16), hot)

    def pair(step, _):
        first, second = eight(2 * step), eight(2 * step + 1)
        place = pl.ds(pl.multiple_of(16 * step, 16), 16)
        for h in range(heights):
            both = jnp.concatenate([first[8 * h : 8 * h + 8], second[8 * h : 8 * h + 8]], axis=0)
            if h < near_heights:
                near[place, h * LANES : (h + 1) * LANES] = both.astype(BF16)
            else:
                at = h - near_heights
                far[place, at * LANES : (at + 1) * LANES] = both.astype(BF16)
        return 0

    lax.fori_loop(0, names.shape[0] // 2, pair, 0, unroll=4)
    out = [copies.start(near, near_hbm), copies.start(far, far_hbm)]
    for copy in got:
        copy.wait()
    count = rows // BLOCK

    def front(step):
        here = rows_of(step)
        own = features[here]
        low = own[:, :lowered]
        is_board = kinds[here] == 1
        boards[here] = jnp.where(is_board, jnp.ones((BLOCK, LANES), F32), 0.0)
        masked[here] = jnp.where(is_board, low, jnp.zeros_like(low))
        left = jnp.where(is_board, dot(low, proj[...]), own.astype(F32)).astype(BF16)
        hidden[here] = left
        pre = dot(left, q_weight[...]) + q_bias[...]
        sigma = sigmoid(pre)
        active[here] = (pre * sigma).astype(BF16)
        slope[here] = sigma + pre * sigma * (1.0 - sigma)

    each_block(count, front)
    out += [copies.start(hidden, hidden_hbm), copies.start(slope, slope_hbm)]
    out += [copies.start(masked, lowered_hbm)]
    got_w.wait()
    agg_out = copies.by_blocks(agg, agg_hbm, start=False)
    base_out = copies.by_blocks(base, base_hbm, start=False)

    def local(step):
        here = rows_of(step)
        agg[here] = dot(near[here], active[...]).astype(BF16)
        agg_out(step).start()
        base[here] = dot(hidden[here], w_top[...]) + w_bias[...]
        base_out(step).start()

    each_block(count, local)
    for copy in out:
        copy.wait()
    each_block(count, lambda step: agg_out(step).wait())
    each_block(count, lambda step: base_out(step).wait())


def combine_kernel(
    live, bits, weight, q_bias, far_hbm, incoming_hbm, proj_hbm, q_hbm, agg_hbm, base_hbm, w_hbm,
    cotangent_hbm, hidden_hbm,
    embedding_hbm, dpre2_hbm, dagg_hbm, to_peers_hbm, w_sent_hbm, w_kept, far_hidden_hbm,
    far_dpre_hbm, far_lowered_hbm, far_slope_hbm, bias,
    far, incoming, proj, q_weight, agg, base, w_low, cotangent, hidden, mean, dpre2, dagg, to_peers,
    w_sent, far_hidden, far_slope, far_lowered, arrived,
):
    copies = Copies(arrived)
    rows, width = agg.shape
    count = rows // BLOCK
    got_front = [copies.start(incoming_hbm, incoming), copies.start(proj_hbm, proj)]
    got_front += [copies.start(q_hbm, q_weight)]
    got = [copies.start(far_hbm, far), copies.start(w_hbm.at[width:], w_low)]
    got_agg = copies.by_blocks(agg_hbm, agg)
    got_base = copies.by_blocks(base_hbm, base)
    got_cotangent = copies.by_blocks(cotangent_hbm, cotangent)
    got_hidden = copies.start(hidden_hbm, hidden)
    embedding = base
    embedding_out = copies.by_blocks(embedding, embedding_hbm, start=False)
    dpre2_out = copies.by_blocks(dpre2, dpre2_hbm, start=False)
    dagg_out = copies.by_blocks(dagg, dagg_hbm, start=False)
    outs = [embedding_out, dpre2_out, dagg_out]
    bias[...] = jnp.zeros(bias.shape, F32)
    for copy in got_front:
        copy.wait()
    lowered = proj.shape[0]
    active = incoming
    held = far_hidden.shape[0] == far.shape[1]

    def move(*pairs):
        for i, (source, target) in enumerate(pairs):
            copy = pltpu.make_async_copy(source, target, arrived.at[arrived.shape[0] - 1 - i])
            copy.start()
            copy.wait()

    def front(step):
        here = rows_of(step)
        spot = here if held else pl.ds(0, BLOCK)
        own = incoming[here]
        is_board = own[:, width - 1 :].astype(F32) > MARK / 2
        low = own[:, :lowered]
        far_lowered[spot] = jnp.where(is_board, low, jnp.zeros_like(low))
        left = jnp.where(is_board, dot(low, proj[...]), own.astype(F32)).astype(BF16)
        far_hidden[spot] = left
        pre = dot(left, q_weight[...]) + q_bias[...]
        sigma = sigmoid(pre)
        active[here] = (pre * sigma).astype(BF16)
        far_slope[spot] = sigma + pre * sigma * (1.0 - sigma)
        if not held:
            move(
                (far_lowered, far_lowered_hbm.at[here]),
                (far_hidden, far_hidden_hbm.at[here]),
                (far_slope, far_slope_hbm.at[here]),
            )

    each_block(far.shape[1] // BLOCK, front)
    far_out = []
    if held:
        far_out += [copies.start(far_hidden, far_hidden_hbm)]
        far_out += [copies.start(far_lowered, far_lowered_hbm)]
    for copy in got:
        copy.wait()

    def node_block(step):
        here = rows_of(step)
        got_agg(step).wait()
        total = agg[here].astype(F32) + dot(far[here], active[...])
        average = (total * weight[here]).astype(BF16)
        mean[here] = average
        got_base(step).wait()
        pre = base[here] + dot(average, w_low[...])
        got_cotangent(step).wait()
        sigma = sigmoid(pre)
        post = pre * sigma
        scale = lax.rsqrt(jnp.sum(post * post, axis=1, keepdims=True) + 1e-06)
        row = lax.broadcasted_iota(jnp.int32, (BLOCK, 1), 0) + step * BLOCK
        scale = jnp.where(row < live[0], scale, 0.0)
        embedding[here] = post * scale
        grad = cotangent[here].astype(F32)
        lean = scale * scale * scale * jnp.sum(post * grad, axis=1, keepdims=True)
        dpost = scale * grad - post * lean
        low = (dpost * (sigma + post * (1.0 - sigma))).astype(BF16)
        dpre2[here] = low
        bias[...] += add_up(low)
        dagg[here] = (contract_cols(low, w_low[...]) * weight[here]).astype(BF16)
        for out in outs:
            out(step).start()

    each_block(count, node_block)
    far_dpre = far_hidden
    if held:
        far_out.pop(0).wait()

    def peer_block(step):
        here = rows_of(step)
        spot = here if held else pl.ds(0, BLOCK)
        if not held:
            move((far_slope_hbm.at[here], far_slope))
        table = contract_rows(far[:, here], dagg[...])
        to_peers[spot] = table.astype(BF16)
        far_dpre[spot] = (table * far_slope[spot]).astype(BF16)
        if not held:
            move((to_peers, to_peers_hbm.at[here]), (far_dpre, far_dpre_hbm.at[here]))

    each_block(far.shape[1] // BLOCK, peer_block)
    if held:
        far_out += [copies.start(to_peers, to_peers_hbm), copies.start(far_dpre, far_dpre_hbm)]
    got_hidden.wait()
    stride = width // PLACES
    for target, target_hbm, mark, low in ((w_sent, w_sent_hbm, 2, 1), (w_kept, None, 1, 0)):

        @pl.when(bits[0] == low)
        def _():
            write_pieces(bits[mark], [(hidden, 0, dpre2)], width, target, stride, 0)

        @pl.when(bits[0] != low)
        def _():
            write_pieces(bits[mark], [(mean, 0, dpre2)], width, target, stride, 0)

        if target_hbm is not None:
            far_out += [copies.start(target, target_hbm)]
    for copy in far_out:
        copy.wait()
    for out in outs:
        each_block(count, lambda step, out=out: out(step).wait())


def write_pieces(mark, pairs, depth, out, stride, at, plus=None):
    piece = depth // PLACES
    size = min(BLOCK, depth)

    def block(step):
        product = 0.0
        for left, first, right in pairs:
            here = pl.ds(pl.multiple_of(first + step * size, size), size)
            product += contract_rows(left[:, here], right[...])
        write_block(mark, product, step * (size // piece), out, stride, at, piece, plus)

    each_block(depth // size, block)


def write_block(mark, product, first, out, stride, at, piece, plus=None):
    for j in range(product.shape[0] // piece):
        place = (first + j) ^ mark
        here = pl.ds(pl.multiple_of(place * stride + at, 16), piece)
        part = product[j * piece : (j + 1) * piece]
        if plus is not None:
            part += plus[here].astype(F32)
        out[here] = part.astype(out.dtype)


def gradients_kernel(
    bits, w_bias, near_hbm, dagg_hbm, slope_hbm, dpre2_hbm, w_hbm, hidden_hbm,
    far_hidden_hbm, far_dpre_hbm, lowered_hbm, far_lowered_hbm, q_hbm,
    dtable_hbm, djoined_hbm, sent_hbm, kept_hbm,
    near, dagg, slope, dpre2, w_top, hidden, far_hidden, far_dpre, lowered, far_lowered,
    q_weight, dtable, djoined, dpre, sent, kept, bias, arrived,
):
    copies = Copies(arrived)
    rows, width = dpre.shape
    depth = lowered.shape[1]
    half = width // 2
    count = rows // BLOCK
    got_table = [copies.start(dagg_hbm, dagg), copies.start(near_hbm, near)]
    got_slope = copies.by_blocks(slope_hbm, slope)
    got_q = [copies.start(hidden_hbm, hidden), copies.start(far_hidden_hbm, far_hidden)]
    got_q += [copies.start(far_dpre_hbm, far_dpre)]
    got_joined = [copies.start(w_hbm.at[:width], w_top), copies.start(dpre2_hbm, dpre2)]
    got_p = [copies.start(lowered_hbm, lowered), copies.start(far_lowered_hbm, far_lowered)]
    got_p += [copies.start(q_hbm, q_weight)]
    bias[...] = jnp.zeros(bias.shape, F32)
    for copy in got_table:
        copy.wait()

    def table_block(step):
        here = rows_of(step)
        table = contract_rows(near[:, here], dagg[...])
        dtable[here] = table.astype(BF16)
        got_slope(step).wait()
        low = (table * slope[here]).astype(BF16)
        dpre[here] = low
        bias[...] += add_up(low)

    each_block(count, table_block)
    out = [copies.start(dtable, dtable_hbm)]
    for copy in got_q:
        copy.wait()

    def far_block(step):
        bias[...] += add_up(far_dpre[rows_of(step)])

    each_block(far_dpre.shape[0] // BLOCK, far_block)
    stride = (half + depth // 2) // PLACES
    sides = ((sent, sent_hbm, 1 - bits[0], bits[2]), (kept, kept_hbm, bits[0], bits[1]))

    def write_q(target, side, mark):
        first = side * half
        pairs = [(hidden, first, dpre), (far_hidden, first, far_dpre)]
        write_pieces(mark, pairs, half, target, stride, 0)

    def write_p(target, side, mark):
        here = pl.ds(pl.multiple_of(side * (depth // 2), depth // 2), depth // 2)
        part = lowered[:, here]
        through = contract_rows(part, dpre[...]) + contract_rows(far_lowered[:, here], far_dpre[...])
        product = contract_cols(through.astype(BF16), q_weight[...])
        product += contract_rows(part, djoined[...])
        write_block(mark, product, 0, target, stride, half // PLACES, depth // 2 // PLACES)

    write_q(sent, *sides[0][2:])
    for copy in got_joined:
        copy.wait()

    def joined_block(step):
        here = rows_of(step)
        djoined[here] = contract_cols(dpre2[here], w_top[...]).astype(BF16)

    each_block(count, joined_block)
    out += [copies.start(djoined, djoined_hbm)]
    for copy in got_p:
        copy.wait()
    write_p(sent, *sides[0][2:])
    row = lax.broadcasted_iota(jnp.int32, (BIAS_ROWS, 1), 0)
    block = jnp.zeros((BIAS_ROWS, width), F32)
    for i, part in enumerate((bias, w_bias)):
        total = jnp.sum(part[...], axis=0, keepdims=True)
        high = total.astype(BF16).astype(F32)
        block = jnp.where(row == i, high, jnp.where(row == i + 2, total - high, block))
    sent[sent.shape[0] - BIAS_ROWS :] = block.astype(BF16)
    out += [copies.start(sent, sent_hbm)]
    write_q(kept, *sides[1][2:])
    write_p(kept, *sides[1][2:])
    out += [copies.start(kept, kept_hbm)]
    for copy in out:
        copy.wait()


def grad_features_kernel(
    send, boards, returned_hbm, dtable_hbm, slope_hbm, q_hbm, djoined_hbm, proj_hbm, grad_hbm,
    returned, dtable, slope, q_weight, djoined, proj, arrived,
):
    copies = Copies(arrived)
    rows = dtable.shape[0]
    lowered = proj.shape[0]
    count = rows // BLOCK
    got = [copies.start(returned_hbm, returned), copies.start(dtable_hbm, dtable)]
    for copy in got:
        copy.wait()
    got_slope = copies.by_blocks(slope_hbm, slope)
    got = [copies.start(q_hbm, q_weight), copies.start(djoined_hbm, djoined)]
    got += [copies.start(proj_hbm, proj)]
    grad_out = copies.by_blocks(slope, grad_hbm, start=False)

    def own_block(step):
        here = rows_of(step)
        row = lax.broadcasted_iota(jnp.int32, (BLOCK, send.shape[1]), 0) + step * BLOCK
        hot = jnp.where(row == send[...], 1.0, 0.0).astype(BF16)
        owned = dtable[here].astype(F32) + dot(hot, returned[...])
        got_slope(step).wait()
        dtable[here] = (owned * slope[here]).astype(BF16)

    each_block(count, own_block)
    for copy in got:
        copy.wait()

    def block(step):
        here = rows_of(step)
        low = contract_cols(dtable[here], q_weight[...]) + djoined[here].astype(F32)
        low = low.astype(BF16)
        product = contract_cols(low, proj[...])
        is_board = boards[here, :1] > 0.5
        own = low.astype(F32)
        slope[here, :lowered] = jnp.where(is_board, product, own[:, :lowered])
        slope[here, lowered:] = jnp.where(is_board, 0.0, own[:, lowered:])
        grad_out(step).start()

    each_block(count, block)
    each_block(count, lambda step: grad_out(step).wait())


def ordered_kernel(bits, held, *refs, count, other):
    outs = refs[-count:]
    mark = bits[2 if other else 1] % 4
    stride = held.shape[0] // 4
    first = 0
    for out in outs:
        piece = out.shape[0] // 4
        for j in range(4):
            here = pl.ds(pl.multiple_of((j ^ mark) * stride + first, 16), piece)
            out[j * piece : (j + 1) * piece] = held[here].astype(F32)
        first += piece


def ordered(bits, held, sizes, other, into=None, part=0, parts=1):
    columns = held.shape[1]
    steps = PLACES // 4
    into = list(into or ())
    mark = 2 if other else 1

    def target(i, b):
        block = (part * (steps // parts) + i) ^ (b[mark] // 4)
        return ((1 - b[0] if other else b[0]) * steps + block, 0)

    return pl.pallas_call(
        functools.partial(ordered_kernel, count=len(sizes), other=other),
        out_shape=[shape((2 * PLACES * size, columns), F32) for size in sizes],
        grid_spec=pltpu.PrefetchScalarGridSpec(
            num_scalar_prefetch=1,
            grid=(steps // parts,),
            in_specs=[pl.BlockSpec((4 * sum(sizes), columns), lambda i, b: (i, 0))]
            + [ANY] * len(into),
            out_specs=[pl.BlockSpec((4 * size, columns), target) for size in sizes],
        ),
        input_output_aliases={2 + i: i for i in range(len(into))},
        compiler_params=pltpu.CompilerParams(vmem_limit_bytes=24 * MEGA),
        cost_estimate=COST,
    )(bits, held, *into)


def swap(value, axis, mask):
    size = lax.axis_size(axis)
    return lax.ppermute(value, axis, [(s, s ^ mask) for s in range(size)])


WAYS = (
    (("dom", 1), ("rep", 2)),
    (("rep", 2), ("dom", 1)),
    (("dom", 2), ("dom", 4)),
    (("dom", 4), ("dom", 2)),
)
FAR_WAYS = WAYS[3], WAYS[2], (("dom", 6), ("dom", 6))


def cross(value, ways):
    doms, reps = lax.axis_size("dom"), lax.axis_size("rep")
    pairs = []
    for d in range(doms):
        for r in range(reps):
            axis, mask = ways[r % 2]
            to = (d ^ mask, r) if axis == "dom" else (d, r ^ mask)
            pairs.append((d * reps + r, to[0] * reps + to[1]))
    return lax.ppermute(value, ("dom", "rep"), pairs)


class Order:
    def __init__(self):
        self.last = ()

    def __call__(self, step, *operands):
        held, _ = lax.optimization_barrier((operands, self.last))
        result = step(*held)
        self.last = jax.tree.leaves(result)[:1]
        return result

    def tick(self):
        def nothing(_, out):
            out[...] = jnp.zeros(out.shape, F32)

        self.last = [
            pl.pallas_call(
                nothing,
                out_shape=shape((8, LANES), F32),
                in_specs=[ANY],
                out_specs=VMEM,
                compiler_params=pltpu.CompilerParams(vmem_limit_bytes=MEGA),
                cost_estimate=COST,
            )(*self.last)
        ]


def pack(bias):
    high = lax.reduce_precision(bias, 8, 7)
    rest = jnp.zeros((BIAS_ROWS - 4, bias.shape[1]), F32)
    return jnp.concatenate([high, bias - high, rest]).astype(BF16)


def unpack(rows):
    rows = rows[-BIAS_ROWS:].astype(F32)
    return rows[:2] + rows[2:4]


def split_kernel(*refs, with_bias):
    held, back = refs[:2]
    away, stay = refs[-2:]
    half = stay.shape[0]
    size = 64

    def block(step):
        here = pl.ds(pl.multiple_of(step * size, size), size)
        there = pl.ds(pl.multiple_of(half + step * size, size), size)
        stay[here] = held[here].astype(F32) + back[here].astype(F32)
        away[here] = (held[there].astype(F32) + back[there].astype(F32)).astype(BF16)

    each_block(half // size, block)
    if with_bias:
        mine = refs[2][...].astype(F32)
        other = back[2 * half :].astype(F32)
        total = mine[0:2] + mine[2:4] + (other[0:2] + other[2:4])
        total = jnp.concatenate([total, total] + [jnp.zeros((12, total.shape[1]), F32)])
        high = total.astype(BF16).astype(F32)
        row = lax.broadcasted_iota(jnp.int32, total.shape, 0)
        rest = jnp.where(row < 4, total - high, 0.0)
        away[half:] = jnp.where(row < 2, high, rest).astype(BF16)


def split(held, back, *mine):
    half, width = held.shape[0] // 2, held.shape[1]
    return pl.pallas_call(
        functools.partial(split_kernel, with_bias=bool(mine)),
        out_shape=(
            shape((half + len(mine) * BIAS_ROWS, width), BF16), shape((half, width), F32)
        ),
        in_specs=[VMEM] * (2 + len(mine)),
        out_specs=(VMEM, VMEM),
        compiler_params=pltpu.CompilerParams(vmem_limit_bytes=16 * MEGA),
        cost_estimate=COST,
    )(held, back, *mine)


class PieceSum:
    def __init__(self, sent, with_bias):
        self.got = swap(sent, "rep", 1)
        self.bias = None
        self.mine = (sent[-BIAS_ROWS:],) if with_bias else ()
        self.stage = 0

    def first(self, order, kept):
        away, self.held = order(split, kept, self.got, *self.mine)
        self.bias = unpack(away) if self.mine else None
        self.back = cross(away, WAYS[0])

    def reduce(self, order):
        self.stage += 1
        self.split(order, self.held, self.back)

    def split(self, order, held, back):
        half = held.shape[0] // 2

        def step(held, back, bias):
            stay = held[:half].astype(F32) + back[:half].astype(F32)
            away = (held[half:].astype(F32) + back[half : 2 * half].astype(F32)).astype(BF16)
            if bias is not None:
                bias = bias + unpack(back)
                away = jnp.concatenate([away, pack(bias)])
                bias = unpack(away)
            return away, stay, bias

        away, self.held, self.bias = order(step, held, back, self.bias)
        self.back = cross(away, WAYS[self.stage])

    def reduce_far(self, order):
        part = self.held.shape[0] // 4

        def step(held, back, bias):
            stay = held[:part] + back[:part].astype(F32)
            if bias is not None:
                bias = bias + unpack(back)
                packed = pack(bias)
                bias = unpack(packed)
            aways = []
            for i in (1, 2, 3):
                here = slice(i * part, (i + 1) * part)
                away = (held[here] + back[here].astype(F32)).astype(BF16)
                aways.append(away if bias is None else jnp.concatenate([away, packed]))
            return aways, stay, bias

        aways, self.held, self.bias = order(step, self.held, self.back, self.bias)
        self.back = [cross(away, way) for away, way in zip(aways, FAR_WAYS)]

    def turn_far(self, order):
        rows = self.held.shape[0]

        def step(held, back, bias):
            total = held + sum(b[:rows].astype(F32) for b in back)
            if bias is not None:
                got = [unpack(b) for b in back]
                bias = (bias + got[0]) + (got[1] + got[2])
            return total.astype(BF16), bias

        total, self.bias = order(step, self.held, self.back, self.bias)
        self.held = self.beyond(total)
        self.back = [cross(self.held, way) for way in FAR_WAYS]

    def gather_far(self, order):
        self.held = order(lambda h, b: jnp.concatenate([h] + list(b)), self.held, self.back)
        self.back = cross(self.held, WAYS[self.stage])

    def beyond(self, total):
        mask = 8
        while mask < lax.axis_size("dom"):
            total = (total.astype(F32) + swap(total, "dom", mask).astype(F32)).astype(BF16)
            if self.bias is not None:
                self.bias = self.bias + swap(self.bias, "dom", mask)
            mask *= 2
        return total

    def turn(self, order):
        rows = self.held.shape[0]

        def step(held, back, bias):
            total = (held + back[:rows].astype(F32)).astype(BF16)
            return total, None if bias is None else bias + unpack(back)

        total, self.bias = order(step, self.held, self.back, self.bias)
        self.held = self.beyond(total)
        self.back = cross(self.held, WAYS[self.stage])

    def gather(self, order):
        self.held = order(lambda *parts: jnp.concatenate(parts), self.held, self.back)
        self.stage -= 1
        self.back = cross(self.held, WAYS[self.stage])

    def last(self, order):
        self.mine = order(lambda *parts: jnp.concatenate(parts), self.held, self.back)
        self.other = swap(self.mine, "rep", 1)

    def gather_last(self, order):
        extra = [] if self.bias is None else [pack(self.bias)]
        rows = self.held.shape[0] + self.back.shape[0]
        self.mine = order(lambda *parts: jnp.concatenate(parts), self.held, self.back, *extra)
        self.stage -= 1
        self.back = cross(self.mine[:rows], WAYS[self.stage])
        self.other = swap(self.mine, "rep", 1)

    def last_half(self, order):
        self.back = order(lambda value: value, self.back)
        self.other_back = swap(self.back, "rep", 1)


def per_device(
    features,
    node_type,
    neighbours,
    importance,
    send_rows,
    live_rows,
    proj_board,
    q_weight,
    q_bias,
    w_weight,
    w_bias,
    cotangent,
):
    rows, width = features.shape
    lowered = proj_board.shape[0]
    halo = send_rows.shape[0]
    slots = importance.shape[1]
    dom = lax.axis_index("dom")
    rep = lax.axis_index("rep")
    core, y, x, z = rep % 2, rep // 2 % 2, dom % 2, dom // 2 % 4
    low_z, high_z = z % 2, z // 2
    marks = x * 8 + y * 4 + low_z * 2 + high_z, y * 8 + x * 4 + high_z * 2 + low_z
    own, sibling = jnp.where(core == 0, marks[0], marks[1]), jnp.where(core == 0, marks[1], marks[0])
    bits = jnp.stack([core, own, sibling]).astype(jnp.int32)
    send_row = send_rows.reshape(1, halo)
    board_row = node_type.reshape(1, rows)
    kinds = node_type.reshape(rows, 1)
    q_bias_row = q_bias.reshape(1, width)
    w_bias_row = w_bias.reshape(1, width)
    low = (rows, width)
    half = width // 2

    def buffers(*dims):
        return [pltpu.VMEM(d, kind) for d, kind in dims]

    def semaphores(count):
        return [pltpu.SemaphoreType.DMA((count,))]

    outgoing = call(
        outgoing_kernel,
        shape((halo, width), BF16),
        [whole(1, halo), whole(1, rows), ANY],
        whole(halo, width),
        buffers((low, BF16)) + semaphores(1),
    )(send_row, board_row, features)
    incoming = lax.all_to_all(outgoing, "dom", split_axis=0, concat_axis=0, tiled=True)

    wide = -(-slots // 64) * 64
    pad = ((0, 0), (0, wide - slots))
    names = jnp.pad(neighbours, pad, constant_values=-1).reshape(rows // 8, 8 * wide)
    weights = jnp.pad(importance, pad).reshape(rows // 8, 8 * wide)
    narrow = (rows, lowered)
    near, far, hidden, slope, agg, base, own_lowered, boards = call(
        local_kernel,
        (shape((rows, rows), BF16), shape((rows, halo), BF16), shape(low, BF16))
        + (shape(low, F32), shape(low, BF16), shape(low, F32))
        + (shape(narrow, BF16), shape((rows, LANES), F32)),
        [whole(rows // 8, 8 * wide)] * 2 + [whole(rows, 1)] + [whole(1, width)] * 2 + [ANY] * 4,
        (ANY,) * 7 + (whole(rows, LANES),),
        buffers((low, BF16), ((lowered, width), BF16), ((width, width), BF16))
        + buffers(((width, width), BF16), ((rows, rows), BF16), ((rows, halo), BF16))
        + buffers((low, BF16), (low, BF16), (low, F32), (low, BF16), (low, F32), (narrow, BF16))
        + semaphores(9 + 2 * (rows // BLOCK)),
        tokens=(outgoing, bits),
    )(names, weights, kinds, q_bias_row, w_bias_row, features, proj_board, q_weight, w_weight)

    weight = (1.0 / jnp.sum(importance, axis=1)).reshape(rows, 1)
    w_dims = (width, width)
    far_low, far_narrow = (halo, width), (halo, lowered)
    spot = halo if halo <= rows else BLOCK
    (
        embedding, dpre2, dagg, to_peers, w_sent, w_kept, far_hidden, far_dpre, far_lowered, _,
        w_bias_part,
    ) = call(
        combine_kernel,
        (shape(low, F32), shape(low, BF16), shape(low, BF16))
        + (shape(far_low, BF16), shape(w_dims, BF16), shape(w_dims, BF16))
        + (shape(far_low, BF16), shape(far_low, BF16), shape(far_narrow, BF16))
        + (shape(far_low if spot < halo else (8, LANES), F32), shape((8, width), F32)),
        [SMEM, SMEM, whole(rows, 1), whole(1, width)] + [ANY] * 9,
        (ANY,) * 5 + (VMEM,) + (ANY,) * 4 + (whole(8, width),),
        buffers(((rows, halo), BF16), (far_low, BF16), ((lowered, width), BF16))
        + buffers(((width, width), BF16), (low, BF16), (low, F32), ((width, width), BF16))
        + buffers((low, BF16), (low, BF16), (low, BF16), (low, BF16), (low, BF16))
        + buffers(((spot, width), BF16), (w_dims, BF16), ((spot, width), BF16))
        + buffers(((spot, width), F32), ((spot, lowered), BF16))
        + semaphores(14 + 6 * (rows // BLOCK)),
        limit=56,
    )(
        live_rows, bits, weight, q_bias_row, far, incoming, proj_board, q_weight, agg, base, w_weight,
        cotangent, hidden,
    )
    returned = lax.all_to_all(to_peers, "dom", split_axis=0, concat_axis=0, tiled=True)

    order = Order()
    w_sum = PieceSum(w_sent, False)
    late_rows = (width + lowered) // 2
    sent_dims, kept_dims = (late_rows + BIAS_ROWS, width), (late_rows, width)
    w_sum.first(order, w_kept)
    dtable, djoined, late_sent, late_kept = order(
        call(
            gradients_kernel,
            (shape(low, BF16), shape(low, BF16))
            + (shape(sent_dims, BF16), shape(kept_dims, BF16)),
            [SMEM, whole(8, width)] + [ANY] * 11,
            (ANY,) * 4,
            buffers(((rows, rows), BF16), (low, BF16), (low, F32), (low, BF16))
            + buffers(((width, width), BF16), (low, BF16), (far_low, BF16))
            + buffers((far_low, BF16), (narrow, BF16), (far_narrow, BF16), ((width, width), BF16))
            + buffers((low, BF16), (low, BF16), (low, BF16), (sent_dims, BF16))
            + buffers((kept_dims, BF16), ((8, width), F32))
            + semaphores(16 + rows // BLOCK),
            moved=200,
        ),
        bits, w_bias_part, near, dagg, slope, dpre2, w_weight, hidden, far_hidden, far_dpre,
        own_lowered, far_lowered, q_weight,
    )
    w_sum.reduce(order)
    late_sum = PieceSum(order(lambda sent: sent, late_sent), True)
    returned = order(lambda value: value, returned)
    late_sum.first(order, late_kept)
    w_sizes, late_sizes = [width // 16], [width // 32, lowered // 32]
    w_sum.reduce(order)
    late_sum.reduce(order)
    w_sum.reduce(order)
    late_sum.reduce(order)
    w_sum.turn(order)
    w_sum.gather(order)
    late_sum.reduce(order)
    late_sum.turn(order)
    w_sum.gather(order)
    late_sum.gather(order)
    late_sum.gather(order)
    w_sum.gather(order)
    grad_features = order(
        call(
            grad_features_kernel,
            shape(low, F32),
            [whole(1, halo), whole(rows, LANES)] + [ANY] * 6,
            ANY,
            buffers((far_low, BF16), (low, BF16), (low, F32), ((width, width), BF16))
            + buffers((low, BF16), ((lowered, width), BF16))
            + semaphores(5 + 2 * (rows // BLOCK)),
            moved=200,
        ),
        send_row, boards, returned, dtable, slope, q_weight, djoined, proj_board,
    )
    late_sum.gather_last(order)
    both = order(
        lambda b, m: ordered(b, m, late_sizes, False, None, 0, 2), bits, late_sum.mine
    )
    w_sum.last(order)
    both = order(
        lambda b, m, o: ordered(b, m, late_sizes, True, o, 0, 2), bits, late_sum.other, both
    )
    grad_w = order(lambda b, m: ordered(b, m, w_sizes, False), bits, w_sum.mine)
    (grad_w,) = order(lambda b, m, o: ordered(b, m, w_sizes, True, o), bits, w_sum.other, grad_w)
    late_sum.last_half(order)
    both = order(
        lambda b, m, o: ordered(b, m, late_sizes, False, o, 1, 2), bits, late_sum.back, both
    )
    grad_q, grad_proj = order(
        lambda b, m, o: ordered(b, m, late_sizes, True, o, 1, 2), bits, late_sum.other_back, both
    )
    biases = unpack(jnp.where(core == 0, late_sum.mine[-BIAS_ROWS:], late_sum.other[-BIAS_ROWS:]))
    return (embedding, grad_features, grad_proj, grad_q, biases[0], grad_w, biases[1])


def solution(mesh):
    placed = (
        P(("dom", "rep"), None),
        P(("dom", "rep")),
        P(("dom", "rep"), None),
        P(("dom", "rep"), None),
        P(("dom", "rep")),
        P(("dom", "rep")),
        P(),
        P(),
        P(),
        P(),
        P(),
        P(("dom", "rep"), None),
    )
    return jax.shard_map(
        per_device,
        mesh=mesh,
        in_specs=placed,
        out_specs=(P(("dom", "rep"), None), P(("dom", "rep"), None), P(), P(), P(), P(), P()),
        check_vma=False,
    )
```
